32 devices in a mesh: ctx: 8 (over z, x), head: 4 (over y, core).
Axes of the slice: x: 2, y: 2, z: 4, core: 2. Of those that a mesh axis runs over, the one named last changes fastest.
Arguments:
- query: bfloat16 [4096, 4096], P('ctx', 'head'), may hold values from -6 to 6
- key: bfloat16 [4096, 4096], P('ctx', 'head'), may hold values from -6 to 6
- value: bfloat16 [4096, 4096], P('ctx', 'head'), may hold values from -1040 to 1040
- log_decay: float32 [32, 4096], P('head', 'ctx'), may hold values from -1.1 to 0
- doc_lengths: int32 [8], replicated, may hold values from 1 to 2048, 4096 in all
- tile_mask: int32 [32, 20], P('ctx'), may hold values 0 or 1
- gain: float32 [4096], P('head'), may hold values from 0.25 to 1.75
Outputs:
- attended: bfloat16 [4096, 4096], P('ctx', 'head')
The draws below stay inside these ranges and needn't reach their ends.
Inputs may be any that keep to these rules, and one draw needn't show every extreme that they name: `doc_lengths`: the documents fill the stream in order and sum to 4096 positions; the longest has exactly 2048 positions. `tile_mask`: row r is a tile of queries; column j names key tile (r // 4 - 4) * 4 + j.
All inputs are finite; a program needn't handle non-finite values. No bound on the sum of `tile_mask` on one device may be relied on, other than what follows from the above.
Results may differ from the reference program's by a relative error of at most 0.005.
Values may be sent and summed in bfloat16 or wider, within the bound.
No kernel may reach another device: no remote copies, remote signals or barrier semaphores. Data moves between devices by JAX's collectives and lax.ppermute only.
A program may use at most 128 MiB of HBM per device.

```python
import math
from functools import partial
import jax
import jax.numpy as jnp
import numpy as np
from jax import lax

HEAD_COUNT = 32
HD = 128
D = 4096
TOK_DEV = 512
BLK = 128
REACH = 4
TOKEN_COUNT = 4096
NDOCS = 8
NBLK = 4
MAXDOC = 2048


def query_key_pair(key):
    query_key = jax.random.fold_in(key, 101)
    keys_key = jax.random.fold_in(key, 202)
    queries = jnp.clip(jax.random.normal(query_key, (TOKEN_COUNT, D), jnp.float32), -6.0, 6.0)
    keys = jnp.clip(jax.random.normal(keys_key, (TOKEN_COUNT, D), jnp.float32), -6.0, 6.0)
    return (queries, keys)


def draw_query(key, part):
    return query_key_pair(key)[0].astype(jnp.bfloat16)


def draw_key(key, part):
    return query_key_pair(key)[1].astype(jnp.bfloat16)


def draw_value(key, part):
    base_key = jax.random.fold_in(key, 11)
    column_key = jax.random.fold_in(key, 12)
    row_key = jax.random.fold_in(key, 13)
    column = jnp.arange(D, dtype=jnp.float32)[None, :] / D
    column_scale = jnp.exp(jax.random.uniform(column_key, (1, D), jnp.float32, 0.0, math.log(10.0)))
    row_scale = jnp.exp(jax.random.uniform(row_key, (TOKEN_COUNT, 1), jnp.float32, 0.0, math.log(10.0)))
    base = jnp.clip(jax.random.normal(base_key, (TOKEN_COUNT, D), jnp.float32), -6.0, 6.0)
    rising = jnp.power(3.0, 0.5 * column)
    return (base * column_scale * row_scale * rising).astype(jnp.bfloat16)


def draw_log_decay(key, part):
    fast_key = jax.random.fold_in(key, 21)
    quick_key = jax.random.fold_in(key, 22)
    slow_key = jax.random.fold_in(key, 23)
    piece_key = jax.random.fold_in(key, 24)
    rough_key = jax.random.fold_in(key, 25)
    spike_random_key = jax.random.fold_in(key, 26)
    drop_key = jax.random.fold_in(key, 27)
    share = 0.5
    fast = jax.random.uniform(fast_key, (HEAD_COUNT, 1), jnp.float32) < share
    quick_rate = jax.random.uniform(quick_key, (HEAD_COUNT, 1), jnp.float32, 1.0 / 50.0, 1.0 / 30.0)
    slow_rate = jax.random.uniform(slow_key, (HEAD_COUNT, 1), jnp.float32, 0.2, 0.9) / (REACH * TOK_DEV)
    decay_speed = jnp.where(fast, quick_rate, slow_rate)
    pieces = TOKEN_COUNT // TOK_DEV
    piece_factor = jnp.exp(jax.random.uniform(piece_key, (HEAD_COUNT, pieces), jnp.float32, math.log(0.35), 0.0))
    token_wise = jnp.repeat(piece_factor, TOK_DEV, axis=1)
    coarse_noise = jax.random.uniform(rough_key, (HEAD_COUNT, TOKEN_COUNT), jnp.float32, 0.5, 1.5)
    spike_amount = jax.random.uniform(spike_random_key, (HEAD_COUNT, TOKEN_COUNT), jnp.float32) < 4.0 / TOKEN_COUNT
    falloff = jnp.log(jax.random.uniform(drop_key, (HEAD_COUNT, TOKEN_COUNT), jnp.float32, 0.37, 0.8))
    return -decay_speed * token_wise * coarse_noise + jnp.where(spike_amount, falloff, 0.0)


def touch_ends(result, stream_key, least, top_value):
    longest = result.shape.index(max(result.shape))
    spots = []
    for shift in (0, 1):
        where = [jax.random.randint(jax.random.fold_in(stream_key, axis), (), 0, length) for axis, length in enumerate(result.shape)]
        where[longest] = (where[longest] + shift) % result.shape[longest]
        spots.append(tuple(where))
    return result.at[spots[0]].set(least).at[spots[1]].set(top_value)


def split_up(count, total, most, skew):
    loads = [(1 << 20) // math.isqrt(grade ** skew) + 1 for grade in range(2, count + 1)]
    surplus, holding = total - most - (count - 1), [1] * (count - 1)
    while surplus > 0:
        movable = [i for i in range(count - 1) if holding[i] < most]
        whole, remaining = sum([loads[i] for i in movable]), surplus
        for i in movable:
            extra = min(most - holding[i], max(1, remaining * loads[i] // whole), surplus)
            holding[i] = holding[i] + extra
            surplus = surplus - extra
    return np.array([most] + holding)


def uneven(stream_key, number_of, total, bound, lean):
    if number_of == 2:
        one = jax.random.randint(stream_key, (), max(1, total - bound), min(bound, total - 1) + 1)
        return jnp.stack([one, total - one])
    tallies = jnp.asarray(split_up(number_of, total, bound, lean), jnp.int32)
    twos = (number_of - 1) // 2
    source_of, sink = tallies[1:1 + 2 * twos:2], tallies[2:2 + 2 * twos:2]
    slack = jnp.minimum(source_of - 1, bound - sink)
    shifted = jax.random.randint(jax.random.fold_in(stream_key, 1), (twos,), 0, 1 << 20) % (slack + 1)
    tallies = tallies.at[1:1 + 2 * twos:2].set(source_of - shifted).at[2:2 + 2 * twos:2].set(sink + shifted)
    return tallies[jax.random.permutation(jax.random.fold_in(stream_key, 2), number_of)]


def setup_inputs(seed: int = 0) -> dict:
    arg_keys = jax.random.split(jax.random.key(seed), 8)
    return {
        "query": draw_query(jax.random.fold_in(arg_keys[7], 71), 0),
        "key": draw_key(jax.random.fold_in(arg_keys[7], 71), 0),
        "value": draw_value(jax.random.fold_in(arg_keys[7], 71), 0),
        "log_decay": draw_log_decay(jax.random.fold_in(arg_keys[7], 71), 0),
        "doc_lengths": uneven(arg_keys[4], NDOCS, TOKEN_COUNT, MAXDOC, 2).astype(jnp.int32),
        "tile_mask": touch_ends((jax.random.randint(arg_keys[5], (TOKEN_COUNT // BLK, (REACH + 1) * NBLK), 0, 4) < 3).astype(jnp.int32), jax.random.fold_in(arg_keys[5], 1), 0, 1),
        "gain": jnp.clip(1.0 + 0.15 * jax.random.normal(arg_keys[6], (D,), jnp.float32), 0.25, 1.75),
    }


def doc_index(ends, positions):
    return lax.optimization_barrier(jnp.sum((ends[None, :] <= positions[:, None]).astype(jnp.int32), axis=1)).astype(jnp.int32)

def block_step(divisor, state, inputs):
    query_rows, key_rows, value_rows, decay_rows, doc_rows, doc_before = inputs
    length = query_rows.shape[0]
    cumul = jnp.cumsum(decay_rows)
    later = lax.broadcasted_iota(jnp.int32, (length, length), 0)
    earlier = lax.broadcasted_iota(jnp.int32, (length, length), 1)
    allowed = (later >= earlier) & (doc_rows[:, None] == doc_rows[None, :])
    weights = jnp.exp(jnp.where(allowed, cumul[:, None] - cumul[None, :], -jnp.inf))
    scores = jnp.dot(query_rows, key_rows.T, preferred_element_type=jnp.float32)
    mixing = (scores * weights / divisor).astype(jnp.bfloat16)
    inner = jnp.dot(mixing, value_rows, preferred_element_type=jnp.float32)
    alive = (doc_rows == doc_before).astype(jnp.float32)
    scaled_query = query_rows.astype(jnp.float32) * (jnp.exp(cumul) * alive / divisor)[:, None]
    carried = jnp.dot(scaled_query, state, precision=lax.Precision.HIGHEST)
    tail = jnp.exp(cumul[-1] - cumul) * (doc_rows == doc_rows[-1]).astype(jnp.float32)
    update = jnp.dot((key_rows.astype(jnp.float32) * tail[:, None]).T, value_rows.astype(jnp.float32), precision=lax.Precision.HIGHEST)
    new_state = jnp.exp(cumul[-1]) * alive[-1] * state + update
    return (new_state, inner + carried)

def linear_branch(query, key, value, log_decay, docs):
    blocks = TOKEN_COUNT // BLK
    divisor = HD * math.sqrt(TOK_DEV)

    def heads_first(array):
        return array.reshape(blocks, BLK, HEAD_COUNT, HD).transpose(2, 0, 1, 3)
    doc_blocks = docs.reshape(blocks, BLK)
    before = jnp.concatenate([docs[:1], docs[:-1]]).reshape(blocks, BLK)[:, 0]

    def one_head(query_head, key_head, value_head, decay_head):
        start_state = jnp.zeros((HD, HD), jnp.float32)
        return lax.scan(partial(block_step, divisor), start_state, (query_head, key_head, value_head, decay_head, doc_blocks, before))[1]
    outputs = jax.vmap(one_head)(heads_first(query), heads_first(key), heads_first(value), log_decay.reshape(HEAD_COUNT, blocks, BLK))
    return outputs.transpose(1, 2, 0, 3).reshape(TOKEN_COUNT, HEAD_COUNT, HD)

def softmax_branch(query, key, value, tile_mask, docs):
    rows = min(512, TOK_DEV)
    padding = REACH * TOK_DEV
    reach_keys = padding + rows
    columns = (REACH + 1) * NBLK
    key_padded = jnp.concatenate([jnp.zeros((padding, D), jnp.bfloat16), key])
    value_padded = jnp.concatenate([jnp.zeros((padding, D), jnp.bfloat16), value])
    docs_padded = jnp.concatenate([jnp.full((padding,), -1, jnp.int32), docs])
    scale = 1.0 / math.sqrt(HD)

    def one_block(index):
        start = (index * rows).astype(jnp.int32)
        query_block = lax.dynamic_slice_in_dim(query, start, rows, 0).reshape(rows, HEAD_COUNT, HD)
        key_block = lax.dynamic_slice_in_dim(key_padded, start, reach_keys, 0).reshape(reach_keys, HEAD_COUNT, HD)
        value_block = lax.dynamic_slice_in_dim(value_padded, start, reach_keys, 0).reshape(reach_keys, HEAD_COUNT, HD)
        query_pos = start + jnp.arange(rows, dtype=jnp.int32)
        key_pos = start - padding + jnp.arange(reach_keys, dtype=jnp.int32)
        query_doc = lax.dynamic_slice_in_dim(docs, start, rows, 0)
        key_doc = lax.dynamic_slice_in_dim(docs_padded, start, reach_keys, 0)
        query_tile = query_pos // BLK
        key_tile = key_pos // BLK
        column = key_tile[None, :] - (query_tile[:, None] // NBLK - REACH) * NBLK
        in_range = (column >= 0) & (column < columns)
        tile_rows = lax.dynamic_slice_in_dim(tile_mask, (start // BLK).astype(jnp.int32), rows // BLK, 0)
        row_tiles = jnp.repeat(tile_rows, BLK, axis=0)
        picked = jnp.take_along_axis(row_tiles, jnp.clip(column, 0, columns - 1), axis=1)
        allowed = (key_pos[None, :] >= 0) & (key_doc[None, :] == query_doc[:, None]) & (key_pos[None, :] <= query_pos[:, None])
        allowed = allowed & (in_range & (picked == 1) | (key_tile[None, :] == query_tile[:, None]))
        scores = jnp.einsum('qhd,khd->hqk', query_block.astype(jnp.float32), key_block.astype(jnp.float32)) * scale
        masked = jnp.where(allowed[None], scores, -jnp.inf)
        top = lax.optimization_barrier(jnp.max(masked, axis=-1, keepdims=True))
        weights = jnp.exp(masked - top)
        total = lax.optimization_barrier(jnp.sum(weights, axis=-1))
        mixed = jnp.einsum('hqk,khd->qhd', weights.astype(jnp.bfloat16).astype(jnp.float32), value_block.astype(jnp.float32))
        return mixed / total.T[:, :, None]
    outputs = lax.map(one_block, jnp.arange(TOKEN_COUNT // rows, dtype=jnp.int32))
    return outputs.reshape(TOKEN_COUNT, HEAD_COUNT, HD)

def reference(query, key, value, log_decay, doc_lengths, tile_mask, gain):
    ends = jnp.cumsum(doc_lengths).astype(jnp.int32)
    docs = doc_index(ends, jnp.arange(TOKEN_COUNT, dtype=jnp.int32))
    linear_out = linear_branch(query, key, value, log_decay, docs)
    soft_out = softmax_branch(query, key, value, tile_mask, docs)
    mixed = (linear_out + soft_out).reshape(TOKEN_COUNT, D)
    inverse = lax.rsqrt(lax.optimization_barrier(jnp.sum(mixed * mixed, axis=1)) / D + 1e-06)
    return (mixed * inverse[:, None] * gain[None, :]).astype(jnp.bfloat16)
```

```python
import math
from functools import partial

import jax
import jax.numpy as jnp
from jax import lax
from jax.experimental import pallas as pl
from jax.experimental.pallas import tpu as pltpu
from jax.sharding import PartitionSpec as P

D = 4096
BLK = 128
REACH = 4
EPSILON = 1e-06
NEG = -1e30
FAR_OFF = 1 << 30
LOG2E = math.log2(math.e)
PER_CHUNK = 2

NT = (((1,), (1,)), ((), ()))
TN = (((0,), (0,)), ((), ()))


def dot(a, b, dims):
    return lax.dot_general(a, b, dims, preferred_element_type=jnp.float32)


def params(mib=48):
    return pltpu.CompilerParams(vmem_limit_bytes=mib * 1024 * 1024)


def shifted(x, by):
    n = lax.axis_size("ctx")
    return lax.ppermute(x, "ctx", [(i, i + by) for i in range(n) if 0 <= i + by < n])


def even_to_odd(x):
    n = lax.axis_size("ctx")
    return lax.ppermute(x, "ctx", [(i, i + 1) for i in range(0, n - 1, 2)])


def odd_to_even(x):
    n = lax.axis_size("ctx")
    return lax.ppermute(x, "ctx", [(i, i - 1) for i in range(1, n, 2)])


def lane_column(block, lane):
    spots = lax.broadcasted_iota(jnp.int32, block.shape, 1)
    return jnp.sum(jnp.where(spots == lane, block, 0.0), axis=1, keepdims=True)


def masked_scores(keys, q, thr_ref, first):
    scores = dot(keys, q, NT)
    row = lax.broadcasted_iota(jnp.int32, (BLK, q.shape[0]), 0)
    parts = []
    for j in range(keys.shape[0] // BLK):
        ok = row >= thr_ref[first + j : first + j + 1, :]
        parts.append(jnp.where(ok, scores[j * BLK : (j + 1) * BLK], NEG))
    return parts


def softmax_of(parts, scale2):
    top = parts[0]
    for p in parts[1:]:
        top = jnp.maximum(top, p)
    top = jnp.max(top, axis=0, keepdims=True) * scale2
    weights = [jnp.exp2(p * scale2 - top) for p in parts]
    total = weights[0]
    for w in weights[1:]:
        total = total + w
    total = jnp.sum(total, axis=0, keepdims=True)
    return top, total, [w.astype(jnp.bfloat16) for w in weights]


def diag_kernel(scale2, divisor, q_ref, k_ref, v_ref, thr_ref, start_ref, cum_ref, cumc_ref, o_ref, top_ref, tot_ref, lin_ref):
    h = pl.program_id(0)
    q, k, v = q_ref[...], k_ref[...], v_ref[...]
    length = q.shape[0]
    scores = dot(k, q, NT)
    row = lax.broadcasted_iota(jnp.int32, (BLK, length), 0)
    col = lax.broadcasted_iota(jnp.int32, (BLK, length), 1)
    cum_row = cum_ref[pl.ds(h, 1), :]
    cum_col = lane_column(cumc_ref[...], h)
    soft, mix = [], []
    for j in range(length // BLK):
        s = scores[j * BLK : (j + 1) * BLK]
        causal = row <= col - j * BLK
        soft.append(jnp.where(causal & (row >= thr_ref[j : j + 1, :]), s, NEG))
        gap = cum_row - cum_col[j * BLK : (j + 1) * BLK]
        ok = causal & (row >= start_ref[0:1, :] - j * BLK)
        decay = jnp.exp(jnp.where(ok, gap, NEG))
        mix.append((s * decay * (1.0 / divisor)).astype(jnp.bfloat16))
    top, total, weights = softmax_of(soft, scale2)
    o_ref[...] = dot(v, jnp.concatenate(weights, axis=0), TN)
    lin_ref[...] = dot(v, jnp.concatenate(mix, axis=0), TN)
    top_ref[pl.ds(h, 1), :] = top
    tot_ref[pl.ds(h, 1), :] = total


def near_scores(q, k2, k1, thr_ref, scale2):
    n = k2.shape[0] // BLK
    parts = masked_scores(k2, q, thr_ref, 0) + masked_scores(k1, q, thr_ref, n)
    top, total, weights = softmax_of(parts, scale2)
    return top, total, jnp.concatenate(weights[:n], axis=0), jnp.concatenate(weights[n:], axis=0)


def far_kernel(scale2, chunk, q_ref, k2_ref, v2_ref, ka_ref, va_ref, kb_ref, vb_ref, thr_ref, w_ref, out_ref):
    h = pl.program_id(0) + chunk * PER_CHUNK
    k1 = ka_ref[...] + kb_ref[...]
    v1 = va_ref[...] + vb_ref[...]
    k2, v2 = k2_ref[...], v2_ref[...]
    length = k2.shape[0]
    top, total, p2, p1 = near_scores(q_ref[...], k2, k1, thr_ref, scale2)
    w = lane_column(w_ref[...], h)
    kw2 = (k2.astype(jnp.float32) * w[:length]).astype(jnp.bfloat16)
    kw1 = (k1.astype(jnp.float32) * w[length:]).astype(jnp.bfloat16)
    o = dot(v2, p2, TN) + dot(v1, p1, TN)
    state = dot(v2, kw2, TN) + dot(v1, kw1, TN)
    hd = o.shape[0]
    out_ref[0:hd, 0:length] = (o * (1.0 / total)).astype(jnp.bfloat16)
    out_ref[0:hd, length:] = state.astype(jnp.bfloat16)
    lse = top + jnp.log(total) * LOG2E
    hi = lse.astype(jnp.bfloat16)
    rest = lse - hi.astype(jnp.float32)
    mid = rest.astype(jnp.bfloat16)
    low = (rest - mid.astype(jnp.float32)).astype(jnp.bfloat16)
    spot = lax.broadcasted_iota(jnp.int32, (16, length), 0)
    zero = jnp.zeros((16, length), jnp.float32)
    stats = jnp.where(
        spot == 0,
        zero + hi.astype(jnp.float32),
        jnp.where(
            spot == 1,
            zero + mid.astype(jnp.float32),
            jnp.where(spot == 2, zero + low.astype(jnp.float32), jnp.where(spot == 3, zero + 1.0, zero)),
        ),
    )
    out_ref[hd:, 0:length] = stats.astype(jnp.bfloat16)
    out_ref[hd:, length:] = jnp.zeros((16, hd), jnp.bfloat16)


def near_kernel(
    scale2, chunk, q_ref, k2_ref, v2_ref, ka_ref, va_ref, kb_ref, vb_ref, thr_ref, pay_ref, coef_ref,
    od_ref, topd_ref, totd_ref, lind_ref, x_ref, on_ref, lse_ref,
):
    i = pl.program_id(0)
    h = i + chunk * PER_CHUNK
    q = q_ref[...]
    hd = q.shape[1]
    length = q.shape[0]
    k1 = ka_ref[...] + kb_ref[...]
    v1 = va_ref[...] + vb_ref[...]
    v2 = v2_ref[...]
    top, total, p2, p1 = near_scores(q, k2_ref[...], k1, thr_ref, scale2)
    o = dot(v2, p2, TN) + dot(v1, p1, TN)
    top_d = topd_ref[pl.ds(h, 1), :]
    new_top = jnp.maximum(top, top_d)
    a, b = jnp.exp2(top - new_top), jnp.exp2(top_d - new_top)
    total = total * a + totd_ref[pl.ds(h, 1), :] * b
    on = (o * a + od_ref[...] * b) * (1.0 / total)
    lin = lind_ref[...] + dot(pay_ref[0:hd, length:], q, NT) * coef_ref[pl.ds(h, 1), :]
    x_ref[...] = lin + on
    on_ref[...] = on
    lse_ref[pl.ds(i, 1), :] = new_top + jnp.log(total) * LOG2E


def merge_kernel(chunk, q_ref, pay_ref, coef_ref, x_ref, on_ref, lse_ref, mixed_ref, sq_ref):
    i = pl.program_id(0)
    h = i + chunk * PER_CHUNK
    q = q_ref[...]
    length, hd = q.shape
    stats = pay_ref[hd:, 0:length].astype(jnp.float32)
    lse_far = stats[0:1] + stats[1:2] + stats[2:3]
    far = pay_ref[0:hd, 0:length].astype(jnp.float32)
    share = 1.0 / (1.0 + jnp.exp2(jnp.minimum(lse_ref[pl.ds(i, 1), :] - lse_far, 120.0)))
    share = jnp.where((lse_far > 0.5 * NEG) & (stats[3:4] > 0.5), share, 0.0)
    lin = dot(pay_ref[0:hd, length:], q, NT) * coef_ref[pl.ds(h, 1), :]
    mixed = x_ref[...] + share * (far - on_ref[...]) + lin
    mixed_ref[...] = mixed

    @pl.when(i == 0)
    def _():
        sq_ref[...] = jnp.zeros_like(sq_ref)

    sq_ref[...] += jnp.sum(mixed * mixed, axis=0, keepdims=True)


def norm_kernel(chunks, *refs):
    mixed_refs, sq_ref, gain_ref, out_ref = refs[:chunks], refs[chunks], refs[chunks + 1], refs[chunks + 2]
    inverse = lax.rsqrt(jnp.sum(sq_ref[...], axis=0, keepdims=True) / D + EPSILON)
    col = 0
    for ref in mixed_refs:
        for i in range(ref.shape[0] // 128):
            part = (ref[i * 128 : (i + 1) * 128, :] * inverse).T
            out_ref[:, col : col + 128] = (part * gain_ref[:, col : col + 128]).astype(jnp.bfloat16)
            col += 128


def on_device(query, key, value, log_decay, doc_lengths, tile_mask, gain):
    length, features = query.shape
    heads = log_decay.shape[0]
    hd = features // heads
    tiles = length // BLK
    chunks = heads // PER_CHUNK
    width = PER_CHUNK * hd
    divisor = hd * math.sqrt(length)
    scale2 = LOG2E / math.sqrt(hd)
    place = lax.axis_index("ctx")
    f32, bf16 = jnp.float32, jnp.bfloat16

    kv = [
        jnp.concatenate([key[:, i * width : (i + 1) * width], value[:, i * width : (i + 1) * width]], axis=1)
        for i in range(chunks)
    ]
    two_back = [shifted(x, 2) for x in kv]
    from_even = [even_to_odd(x) for x in kv]
    q_far = shifted(query, -2)
    from_odd = [odd_to_even(x) for x in two_back]

    ends = jnp.cumsum(doc_lengths)
    begin = place * length

    def doc_start(pos):
        return jnp.max(jnp.where(ends[:, None] <= pos[None, :], ends[:, None], 0), axis=0)

    local = jnp.arange(length, dtype=jnp.int32)
    start = doc_start(begin + local) - begin
    entry = doc_start(jnp.reshape(begin - 1, (1,)))[0] - begin
    picked = jnp.repeat(tile_mask.T, BLK, axis=1) == 1
    own = jnp.arange(tiles)[:, None] == (local // BLK)[None, :]
    reach = (REACH + 1) * tiles
    bases = (jnp.arange(reach, dtype=jnp.int32) - REACH * tiles) * BLK
    keep = picked.at[REACH * tiles :].set(picked[REACH * tiles :] | own)
    thr = jnp.where(keep, start[None, :] - bases[:, None], FAR_OFF)
    thr_far = shifted(thr[: 2 * tiles], -2)
    thr_near = thr[2 * tiles : 4 * tiles]
    thr_own = thr[4 * tiles :]

    cum = jnp.cumsum(log_decay, axis=1)
    alive = (start < 0).astype(f32)
    coef = jnp.exp(cum) * alive[None, :] * (1.0 / divisor)
    gathered = lax.all_gather(log_decay, "ctx")
    before = lax.dynamic_slice_in_dim(
        jnp.concatenate([jnp.zeros((2,) + log_decay.shape, f32), gathered]), place, 2, 0
    )
    before = before.transpose(1, 0, 2).reshape(heads, 2 * length)
    back = jnp.cumsum(before[:, ::-1], axis=1)[:, ::-1]
    since = jnp.arange(-2 * length, 0, dtype=jnp.int32) >= entry
    weight = (jnp.exp(back - before) * since[None, :].astype(f32)).T
    through = jnp.exp(back[:, 0]) * (entry < -2 * length).astype(f32)
    coef_far = coef * through[:, None]

    whole = lambda *shape: pl.BlockSpec(shape, lambda h: (0,) * len(shape))
    head_cols = pl.BlockSpec((length, hd), lambda h: (0, h))
    head_rows = pl.BlockSpec((hd, length), lambda h: (h, 0))
    o_diag, top_diag, tot_diag, lin_diag = pl.pallas_call(
        partial(diag_kernel, scale2, divisor),
        grid=(heads,),
        in_specs=[head_cols] * 3
        + [whole(tiles, length), whole(1, length), whole(heads, length), whole(length, heads)],
        out_specs=[head_rows, whole(heads, length), whole(heads, length), head_rows],
        out_shape=[
            jax.ShapeDtypeStruct((features, length), f32),
            jax.ShapeDtypeStruct((heads, length), f32),
            jax.ShapeDtypeStruct((heads, length), f32),
            jax.ShapeDtypeStruct((features, length), f32),
        ],
        compiler_params=params(),
        cost_estimate=pl.CostEstimate(flops=6 * heads * length * length * hd, bytes_accessed=8 << 20, transcendentals=2 * heads * length * length),
        name="own_piece",
    )(query, key, value, thr_own, start[None, :], cum, cum.T)

    first = pl.BlockSpec((length, hd), lambda h: (0, h))
    second = pl.BlockSpec((length, hd), lambda h: (0, h + PER_CHUNK))
    pay_rows, pay_cols = hd + 16, length + hd
    pay_spec = pl.BlockSpec((pay_rows, pay_cols), lambda h: (h, 0))
    pair_cost = pl.CostEstimate(flops=8 * PER_CHUNK * length * length * hd, bytes_accessed=3 << 20, transcendentals=2 * PER_CHUNK * length * length)
    sent, merged_in = [], []
    for i in range(chunks):
        q_spec = pl.BlockSpec((length, hd), lambda h, i=i: (0, h + i * PER_CHUNK))
        row_spec = pl.BlockSpec((hd, length), lambda h, i=i: (h + i * PER_CHUNK, 0))
        kv_specs = [first, second] * 3
        kv_args = (two_back[i], two_back[i], from_even[i], from_even[i], from_odd[i], from_odd[i])
        pay = pl.pallas_call(
            partial(far_kernel, scale2, i),
            grid=(PER_CHUNK,),
            in_specs=[q_spec] + kv_specs + [whole(2 * tiles, length), whole(2 * length, heads)],
            out_specs=pay_spec,
            out_shape=jax.ShapeDtypeStruct((PER_CHUNK * pay_rows, pay_cols), bf16),
            compiler_params=params(),
            cost_estimate=pair_cost,
            name="far_pieces",
        )(q_far, *kv_args, thr_far, weight)
        sent.append(shifted(pay, 2))
        x, on, lse = pl.pallas_call(
            partial(near_kernel, scale2, i),
            grid=(PER_CHUNK,),
            in_specs=[q_spec]
            + kv_specs
            + [whole(2 * tiles, length), pay_spec, whole(heads, length), row_spec, whole(heads, length), whole(heads, length), row_spec],
            out_specs=[head_rows, head_rows, whole(PER_CHUNK, length)],
            out_shape=[
                jax.ShapeDtypeStruct((width, length), f32),
                jax.ShapeDtypeStruct((width, length), f32),
                jax.ShapeDtypeStruct((PER_CHUNK, length), f32),
            ],
            compiler_params=params(),
            cost_estimate=pair_cost,
            name="near_pieces",
        )(query, *kv_args, thr_near, pay, coef, o_diag, top_diag, tot_diag, lin_diag)
        merged_in.append((x, on, lse))
    mixed, squares = [], []
    for i in range(chunks):
        q_spec = pl.BlockSpec((length, hd), lambda h, i=i: (0, h + i * PER_CHUNK))
        m, s = pl.pallas_call(
            partial(merge_kernel, i),
            grid=(PER_CHUNK,),
            in_specs=[q_spec, pay_spec, whole(heads, length), head_rows, head_rows, whole(PER_CHUNK, length)],
            out_specs=[head_rows, whole(1, length)],
            out_shape=[jax.ShapeDtypeStruct((width, length), f32), jax.ShapeDtypeStruct((1, length), f32)],
            compiler_params=params(),
            cost_estimate=pl.CostEstimate(flops=1 << 26, bytes_accessed=2 << 20, transcendentals=1024),
            name="merge",
        )(query, sent[i], coef_far, *merged_in[i])
        mixed.append(m)
        squares.append(s)
    total = squares[0]
    for s in squares[1:]:
        total = total + s
    ranks = lax.axis_size("head")
    everyone = lax.all_gather(total.reshape(length // 128, 128), "head").reshape(ranks, length)
    return pl.pallas_call(
        partial(norm_kernel, chunks),
        out_shape=jax.ShapeDtypeStruct((length, features), bf16),
        compiler_params=params(),
        name="normalize",
    )(*mixed, everyone, gain[None, :])


def solution(mesh):
    placed = (
        P("ctx", "head"),
        P("ctx", "head"),
        P("ctx", "head"),
        P("head", "ctx"),
        P(),
        P("ctx", None),
        P("head"),
    )
    return jax.shard_map(on_device, mesh=mesh, in_specs=placed, out_specs=P("ctx", "head"), check_vma=False)
```

```python
import math
from functools import partial

import jax
import jax.numpy as jnp
from jax import lax
from jax.experimental import pallas as pl
from jax.experimental.pallas import tpu as pltpu
from jax.sharding import PartitionSpec as P

D = 4096
BLK = 128
REACH = 4
EPSILON = 1e-06
NEG = -1e30
FAR_OFF = 1 << 30
LOG2E = math.log2(math.e)
PER_CHUNK = 2

NT = (((1,), (1,)), ((), ()))
TN = (((0,), (0,)), ((), ()))


def dot(a, b, dims):
    return lax.dot_general(a, b, dims, preferred_element_type=jnp.float32)


def params(mib=48):
    return pltpu.CompilerParams(vmem_limit_bytes=mib * 1024 * 1024)


def shifted(x, by):
    n = lax.axis_size("ctx")
    return lax.ppermute(x, "ctx", [(i, i + by) for i in range(n) if 0 <= i + by < n])


def even_to_odd(x):
    n = lax.axis_size("ctx")
    return lax.ppermute(x, "ctx", [(i, i + 1) for i in range(0, n - 1, 2)])


def odd_to_even(x):
    n = lax.axis_size("ctx")
    return lax.ppermute(x, "ctx", [(i, i - 1) for i in range(1, n, 2)])


def split3(x):
    hi = x.astype(jnp.bfloat16)
    rest = x - hi.astype(jnp.float32)
    mid = rest.astype(jnp.bfloat16)
    low = (rest - mid.astype(jnp.float32)).astype(jnp.bfloat16)
    return hi.astype(jnp.float32), mid.astype(jnp.float32), low.astype(jnp.float32)


def join3(rows, first):
    return rows[first : first + 1] + rows[first + 1 : first + 2] + rows[first + 2 : first + 3]


def stack_rows(rows, count, length):
    spot = lax.broadcasted_iota(jnp.int32, (count, length), 0)
    out = jnp.zeros((count, length), jnp.float32)
    for i, r in enumerate(rows):
        out = jnp.where(spot == i, r, out)
    return out


def lane_column(block, lane):
    spots = lax.broadcasted_iota(jnp.int32, block.shape, 1)
    return jnp.sum(jnp.where(spots == lane, block, 0.0), axis=1, keepdims=True)


def softmax_of(parts, scale2):
    top = parts[0]
    for p in parts[1:]:
        top = jnp.maximum(top, p)
    top = jnp.max(top, axis=0, keepdims=True) * scale2
    weights = [jnp.exp2(p * scale2 - top) for p in parts]
    total = weights[0]
    for w in weights[1:]:
        total = total + w
    total = jnp.sum(total, axis=0, keepdims=True)
    return top, total, [w.astype(jnp.bfloat16) for w in weights]


def prep_kernel(divisor, place_ref, docs_ref, mask_ref, ld_ref, k_ref, v_ref, thr_ref, start_ref, cum_ref, cumt_ref, coef_ref, dec_ref, entry_ref, pay_ref, token_ref):
    heads, length = ld_ref.shape
    tiles = length // BLK
    begin = place_ref[0] * length
    f32, bf16 = jnp.float32, jnp.bfloat16
    parts = jnp.concatenate(split3(ld_ref[...]), axis=0).astype(bf16)
    u = lax.broadcasted_iota(jnp.int32, (length, length), 0)
    t = lax.broadcasted_iota(jnp.int32, (length, length), 1)
    ones = jnp.where(u <= t, 1.0, 0.0).astype(bf16)
    sums = lax.dot_general(parts, ones, (((1,), (0,)), ((), ())), preferred_element_type=f32)
    cum = sums[:heads] + sums[heads : 2 * heads] + sums[2 * heads :]
    cum_ref[...] = cum
    cumt_ref[...] = jnp.concatenate([cum, jnp.zeros((BLK - heads, length), f32)], axis=0).T
    pos = begin + lax.broadcasted_iota(jnp.int32, (8, length), 1)
    start = jnp.zeros((8, length), jnp.int32)
    end = jnp.int32(0)
    entry = jnp.int32(0)
    for d in range(docs_ref.shape[0]):
        end = end + docs_ref[d]
        start = jnp.where(pos >= end, end, start)
        entry = jnp.where(begin - 1 >= end, end, entry)
    start = start - begin
    start_ref[...] = start
    entry_ref[0] = entry - begin
    coef_ref[...] = jnp.exp(cum) * jnp.where(start[:1] < 0, 1.0 / divisor, 0.0)
    tile_of = lax.broadcasted_iota(jnp.int32, (1, length), 1) // BLK
    reach = mask_ref.shape[1]
    for j in range(reach):
        keep = tile_of < 0
        for i in range(tiles):
            here = mask_ref[i, j] == 1
            if j == REACH * tiles + i:
                here = here | True
            keep = keep | ((tile_of == i) & here)
        base = (j - REACH * tiles) * BLK
        thr_ref[j : j + 1, :] = jnp.where(keep, start[:1] - base, FAR_OFF)
    last = cum[:, length - 1 :]
    chunks = heads // PER_CHUNK
    decs = []
    for c in range(chunks):
        rows = []
        for h in range(c * PER_CHUNK, (c + 1) * PER_CHUNK):
            rows += list(split3(last[h : h + 1] - cum[h : h + 1]))
        for h in range(c * PER_CHUNK, (c + 1) * PER_CHUNK):
            rows += list(split3(last[h : h + 1] + jnp.zeros((1, length), f32)))
        decs.append(stack_rows(rows, 16, length).astype(bf16))
        dec_ref[c * 16 : (c + 1) * 16, :] = decs[-1]
    half = k_ref.shape[1]
    pay_ref[0:length, 0:half] = k_ref[...]
    pay_ref[0:length, half:] = v_ref[...]
    pay_ref[length:, :] = decs[0]
    token_ref[...] = jnp.zeros_like(token_ref)


def pack_kernel(token_in, k_ref, v_ref, dec_ref, *refs):
    pays, token_ref = refs[:-1], refs[-1]
    length = k_ref.shape[0]
    half = PER_CHUNK * 128
    for c, pay in enumerate(pays, 1):
        pay[0:length, 0:half] = k_ref[:, c * half : (c + 1) * half]
        pay[0:length, half:] = v_ref[:, c * half : (c + 1) * half]
        pay[length:, :] = dec_ref[c * 16 : (c + 1) * 16, :]
    token_ref[...] = jnp.zeros_like(token_ref)


def own_kernel(scale2, divisor, base, token_in, q_ref, k_ref, v_ref, thr_ref, start_ref, cum_ref, cumt_ref, o_ref, top_ref, tot_ref, lin_ref, token_ref):
    i = pl.program_id(0)
    h = i + base
    q, k, v = q_ref[...], k_ref[...], v_ref[...]
    length = q.shape[0]
    scores = dot(k, q, NT)
    row = lax.broadcasted_iota(jnp.int32, (BLK, length), 0)
    col = lax.broadcasted_iota(jnp.int32, (BLK, length), 1)
    cum_row = cum_ref[pl.ds(h, 1), :]
    cum_col = lane_column(cumt_ref[...], h)
    soft, mix = [], []
    for j in range(length // BLK):
        s = scores[j * BLK : (j + 1) * BLK]
        causal = row <= col - j * BLK
        soft.append(jnp.where(causal & (row >= thr_ref[j : j + 1, :]), s, NEG))
        gap = cum_row - cum_col[j * BLK : (j + 1) * BLK]
        ok = causal & (row >= start_ref[0:1, :] - j * BLK)
        decay = jnp.exp(jnp.where(ok, gap, NEG))
        mix.append((s * decay * (1.0 / divisor)).astype(jnp.bfloat16))
    top, total, weights = softmax_of(soft, scale2)
    o_ref[...] = dot(v, jnp.concatenate(weights, axis=0), TN)
    lin_ref[...] = dot(v, jnp.concatenate(mix, axis=0), TN)
    top_ref[pl.ds(i, 1), :] = top
    tot_ref[pl.ds(i, 1), :] = total
    token_ref[...] = jnp.zeros_like(token_ref)


class Pieces:
    def __init__(self, two, even, odd, entry):
        self.two, self.even, self.odd, self.entry = two, even, odd, entry
        self.length = two.shape[0] - 16
        rows2 = two[self.length :, :].astype(jnp.float32)
        rows1 = (even[self.length :, :] + odd[self.length :, :]).astype(jnp.float32)
        n = PER_CHUNK
        self.tot1 = [join3(rows1, 3 * n + 3 * i) for i in range(n)]
        self.tot2 = [join3(rows2, 3 * n + 3 * i) for i in range(n)]
        after1 = [join3(rows1, 3 * i) for i in range(n)]
        after2 = [join3(rows2, 3 * i) + self.tot1[i] for i in range(n)]
        col = lax.broadcasted_iota(jnp.int32, (1, self.length), 1)
        w1 = [jnp.where(col - self.length >= entry, jnp.exp(x), 0.0) for x in after1]
        w2 = [jnp.where(col - 2 * self.length >= entry, jnp.exp(x), 0.0) for x in after2]
        self.weight = stack_rows(w1 + w2, BLK, self.length).T

    def keys(self, i):
        cols = slice(i * 128, (i + 1) * 128)
        return self.two[0 : self.length, cols], self.even[0 : self.length, cols] + self.odd[0 : self.length, cols]

    def values(self, i):
        lo = (PER_CHUNK + i) * 128
        cols = slice(lo, lo + 128)
        return self.two[0 : self.length, cols], self.even[0 : self.length, cols] + self.odd[0 : self.length, cols]

    def attend(self, i, q, thr_ref, scale2):
        tiles = self.length // BLK
        k2, k1 = self.keys(i)
        v2, v1 = self.values(i)
        row = lax.broadcasted_iota(jnp.int32, (BLK, q.shape[0]), 0)
        parts = []
        for first, keys in ((0, k2), (tiles, k1)):
            scores = dot(keys, q, NT)
            for j in range(tiles):
                ok = row >= thr_ref[first + j : first + j + 1, :]
                parts.append(jnp.where(ok, scores[j * BLK : (j + 1) * BLK], NEG))
        top, total, weights = softmax_of(parts, scale2)
        o = dot(v2, jnp.concatenate(weights[:tiles], axis=0), TN) + dot(v1, jnp.concatenate(weights[tiles:], axis=0), TN)
        n = PER_CHUNK
        kw1 = (k1.astype(jnp.float32) * self.weight[:, i : i + 1]).astype(jnp.bfloat16)
        kw2 = (k2.astype(jnp.float32) * self.weight[:, n + i : n + i + 1]).astype(jnp.bfloat16)
        state = dot(v2, kw2, TN) + dot(v1, kw1, TN)
        return top, total, o, state.astype(jnp.bfloat16)


def far_kernel(scale2, groups, *refs):
    token_in, entry_ref, q_ref, thr_ref = refs[:4]
    out_ref, token_ref = refs[-2:]
    n = 0
    for g in range(groups):
        two, even, odd = refs[4 + 3 * g : 7 + 3 * g]
        p = Pieces(two, even, odd, entry_ref[0])
        length = p.length
        for i in range(PER_CHUNK):
            top, total, o, state = p.attend(i, q_ref[:, n * 128 : (n + 1) * 128], thr_ref, scale2)
            r = n * 144
            out_ref[r : r + 128, 0:length] = (o * (1.0 / total)).astype(jnp.bfloat16)
            out_ref[r : r + 128, length:] = state
            lse = top + jnp.log(total) * LOG2E
            stats = stack_rows(list(split3(lse)) + [jnp.ones_like(lse)], 16, length)
            out_ref[r + 128 : r + 144, 0:length] = stats.astype(jnp.bfloat16)
            out_ref[r + 128 : r + 144, length:] = jnp.zeros((16, 128), jnp.bfloat16)
            n += 1
    token_ref[...] = jnp.zeros_like(token_ref)


def near_kernel(scale2, chunk, base, token_in, entry_ref, q_ref, thr_ref, coef_ref, two, even, odd, od_ref, topd_ref, totd_ref, lind_ref, x_ref, on_ref, st_ref, token_ref):
    p = Pieces(two, even, odd, entry_ref[0])
    length = p.length
    lses, coefs = [], []
    for i in range(PER_CHUNK):
        h = chunk * PER_CHUNK + i
        q = q_ref[:, i * 128 : (i + 1) * 128]
        rows = slice(i * 128, (i + 1) * 128)
        top, total, o, state = p.attend(i, q, thr_ref, scale2)
        top_d = topd_ref[h - base : h - base + 1, :]
        new_top = jnp.maximum(top, top_d)
        a, b = jnp.exp2(top - new_top), jnp.exp2(top_d - new_top)
        total = total * a + totd_ref[h - base : h - base + 1, :] * b
        inv = 1.0 / total
        on = o * (a * inv) + od_ref[rows, :] * (b * inv)
        coef = coef_ref[h : h + 1, :]
        x_ref[rows, :] = lind_ref[rows, :] + dot(state, q, NT) * coef + on
        on_ref[rows, :] = on
        lses.append(new_top + jnp.log(total) * LOG2E)
        through = jnp.where(entry_ref[0] < -2 * length, jnp.exp(p.tot1[i] + p.tot2[i]), 0.0)
        coefs.append(coef * through)
    st_ref[...] = stack_rows(lses + coefs, 8, length)
    token_ref[...] = jnp.zeros_like(token_ref)


def merge_kernel(groups, token_in, q_ref, pay_ref, *refs):
    mixed_ref, sq_ref, token_ref = refs[-3:]
    squares = None
    n = 0
    for g in range(groups):
        x_ref, on_ref, st_ref = refs[3 * g : 3 * g + 3]
        for i in range(PER_CHUNK):
            q = q_ref[:, n * 128 : (n + 1) * 128]
            length = q.shape[0]
            r = n * 144
            rows = slice(i * 128, (i + 1) * 128)
            stats = pay_ref[r + 128 : r + 144, 0:length].astype(jnp.float32)
            lse_far = join3(stats, 0)
            far = pay_ref[r : r + 128, 0:length].astype(jnp.float32)
            share = 1.0 / (1.0 + jnp.exp2(jnp.minimum(st_ref[i : i + 1, :] - lse_far, 120.0)))
            share = jnp.where((lse_far > 0.5 * NEG) & (stats[3:4] > 0.5), share, 0.0)
            lin = dot(pay_ref[r : r + 128, length:], q, NT) * st_ref[PER_CHUNK + i : PER_CHUNK + i + 1, :]
            mixed = x_ref[rows, :] + share * (far - on_ref[rows, :]) + lin
            mixed_ref[n * 128 : (n + 1) * 128, :] = mixed
            part = jnp.sum(mixed * mixed, axis=0, keepdims=True)
            squares = part if squares is None else squares + part
            n += 1
    sq_ref[...] = squares
    token_ref[...] = jnp.zeros_like(token_ref)


def norm_kernel(parts, *refs):
    mixed_refs, sq_ref, gain_ref, out_ref = refs[:parts], refs[parts], refs[parts + 1], refs[parts + 2]
    inverse = lax.rsqrt(jnp.sum(sq_ref[...], axis=0, keepdims=True) / D + EPSILON)
    col = 0
    for ref in mixed_refs:
        for i in range(ref.shape[0] // 128):
            part = (ref[i * 128 : (i + 1) * 128, :] * inverse).T
            out_ref[:, col : col + 128] = (part * gain_ref[:, col : col + 128]).astype(jnp.bfloat16)
            col += 128


def on_device(query, key, value, log_decay, doc_lengths, tile_mask, gain):
    length, features = query.shape
    heads = log_decay.shape[0]
    hd = features // heads
    tiles = length // BLK
    chunks = heads // PER_CHUNK
    width = PER_CHUNK * hd
    divisor = hd * math.sqrt(length)
    scale2 = LOG2E / math.sqrt(hd)
    place = lax.axis_index("ctx").astype(jnp.int32).reshape(1)
    f32, bf16 = jnp.float32, jnp.bfloat16
    shape = jax.ShapeDtypeStruct
    token_shape = shape((8, 128), f32)
    smem = pl.BlockSpec(memory_space=pltpu.SMEM)
    vmem = pl.BlockSpec(memory_space=pltpu.VMEM)
    loose = pl.BlockSpec(memory_space=pl.ANY)

    def cost(us):
        return pl.CostEstimate(flops=0, bytes_accessed=int(us * 3.69e6), transcendentals=0)

    def cols(first, count):
        return pl.BlockSpec((length, count), lambda *_: (0, first))

    q_far = shifted(query, -2)
    kv_rows = length + 16
    thr, start, cum, cum_t, coef, dec, entry, pay0, token = pl.pallas_call(
        partial(prep_kernel, divisor),
        grid=(1,),
        in_specs=[smem, smem, smem, vmem, cols(0, width), cols(0, width)],
        out_specs=[vmem] * 6 + [smem] + [vmem] * 2,
        out_shape=[
            shape(((REACH + 1) * tiles, length), jnp.int32),
            shape((8, length), jnp.int32),
            shape((heads, length), f32),
            shape((length, BLK), f32),
            shape((heads, length), f32),
            shape((16 * chunks, length), bf16),
            shape((1,), jnp.int32),
            shape((kv_rows, 2 * width), bf16),
            token_shape,
        ],
        compiler_params=params(),
        cost_estimate=cost(2),
        name="prep",
    )(place, doc_lengths, tile_mask, log_decay, key, value)
    packed = pl.pallas_call(
        pack_kernel,
        in_specs=[loose] + [vmem] * 3,
        out_specs=[vmem] * chunks,
        out_shape=[shape((kv_rows, 2 * width), bf16)] * (chunks - 1) + [token_shape],
        compiler_params=params(),
        cost_estimate=cost(3),
        name="pack",
    )(token, key, value, dec)
    token = packed[-1]
    kv = [pay0] + list(packed[:-1])
    two_back, from_even, from_odd = [], [], []
    for x in kv:
        two_back.append(shifted(x, 2))
        from_even.append(even_to_odd(x))
    thr_far = shifted(thr[: 2 * tiles], -2)
    thr_near = thr[2 * tiles : 4 * tiles]
    thr_own = thr[4 * tiles :]
    for x in two_back:
        from_odd.append(odd_to_even(x))

    half = max(PER_CHUNK, heads // 2)
    own = []
    for base in range(0, heads, half):
        whole = lambda *s: pl.BlockSpec(s, lambda h: (0,) * len(s))
        head_cols = pl.BlockSpec((length, hd), lambda h, base=base: (0, h + base))
        head_rows = pl.BlockSpec((hd, length), lambda h: (h, 0))
        *result, token = pl.pallas_call(
            partial(own_kernel, scale2, divisor, base),
            grid=(half,),
            in_specs=[loose]
            + [head_cols] * 3
            + [whole(tiles, length), whole(8, length), whole(heads, length), whole(length, BLK)],
            out_specs=[head_rows, whole(half, length), whole(half, length), head_rows, whole(8, 128)],
            out_shape=[
                shape((half * hd, length), f32),
                shape((half, length), f32),
                shape((half, length), f32),
                shape((half * hd, length), f32),
                token_shape,
            ],
            compiler_params=params(),
            cost_estimate=cost(half * 1.1),
            name="own_piece",
        )(token, query, key, value, thr_own, start, cum, cum_t)
        own.append((base, result))

    def near(c, token):
        base, (o_d, top_d, tot_d, lin_d) = own[c * PER_CHUNK // half]
        rows = pl.BlockSpec((width, length), lambda *_: (c - base // PER_CHUNK, 0))
        x, on, st, token = pl.pallas_call(
            partial(near_kernel, scale2, c, base),
            grid=(1,),
            in_specs=[loose, smem, cols(c, width), vmem, vmem, vmem, vmem, vmem, rows, vmem, vmem, rows],
            out_specs=[vmem] * 4,
            out_shape=[shape((width, length), f32), shape((width, length), f32), shape((8, length), f32), token_shape],
            compiler_params=params(),
            cost_estimate=cost(4),
            name="near_pieces",
        )(token, entry, query, thr_near, coef, two_back[c], from_even[c], from_odd[c], o_d, top_d, tot_d, lin_d)
        return (x, on, st), token

    def far(first, groups, token):
        args = []
        for c in range(first, first + groups):
            args += [two_back[c], from_even[c], from_odd[c]]
        pay, token = pl.pallas_call(
            partial(far_kernel, scale2, groups),
            grid=(1,),
            in_specs=[loose, smem, cols(first // groups, groups * width), vmem] + [vmem] * len(args),
            out_specs=[vmem] * 2,
            out_shape=[shape((groups * PER_CHUNK * 144, length + hd), bf16), token_shape],
            compiler_params=params(),
            cost_estimate=cost(4 * groups),
            name="far_pieces",
        )(token, entry, q_far, thr_far, *args)
        return shifted(pay, 2), token

    def merge(first, groups, pay, parts, token):
        args = []
        for c in range(first, first + groups):
            args += list(parts[c])
        return pl.pallas_call(
            partial(merge_kernel, groups),
            grid=(1,),
            in_specs=[loose, cols(first // groups, groups * width), vmem] + [vmem] * len(args),
            out_specs=[vmem] * 3,
            out_shape=[shape((groups * width, length), f32), shape((1, length), f32), token_shape],
            compiler_params=params(),
            cost_estimate=cost(1.5 * groups),
            name="merge",
        )(token, query, pay, *args)

    plan = [(0, chunks // 2)] + [(c, 1) for c in range(chunks // 2, chunks)]
    parts, pays = {}, []
    for first, groups in plan:
        if first == 0:
            for c in range(groups):
                parts[c], token = near(c, token)
            pay, token = far(first, groups, token)
        else:
            pay, token = far(first, groups, token)
            parts[first], token = near(first, token)
        pays.append(pay)
    mixed, total = [], None
    for (first, groups), pay in zip(plan, pays):
        m, s, token = merge(first, groups, pay, parts, token)
        mixed.append(m)
        total = s if total is None else total + s
    ranks = lax.axis_size("head")
    everyone = lax.all_gather(total.reshape(length // 128, 128), "head").reshape(ranks, length)
    return pl.pallas_call(
        partial(norm_kernel, len(mixed)),
        out_shape=shape((length, features), bf16),
        compiler_params=params(),
        name="normalize",
    )(*mixed, everyone, gain[None, :])


def solution(mesh):
    placed = (
        P("ctx", "head"),
        P("ctx", "head"),
        P("ctx", "head"),
        P("head", "ctx"),
        P(),
        P("ctx", None),
        P("head"),
    )
    return jax.shard_map(on_device, mesh=mesh, in_specs=placed, out_specs=P("ctx", "head"), check_vma=False)
```

```python
import math
from functools import partial

import jax
import jax.numpy as jnp
from jax import lax
from jax.experimental import pallas as pl
from jax.experimental.pallas import tpu as pltpu
from jax.sharding import PartitionSpec as P

D = 4096
BLK = 128
REACH = 4
EPSILON = 1e-06
NEG = -1e30
FAR_OFF = 1 << 30
LOG2E = math.log2(math.e)

NT = (((1,), (1,)), ((), ()))
TN = (((0,), (0,)), ((), ()))
NN = (((1,), (0,)), ((), ()))


def dot(a, b, dims):
    return lax.dot_general(a, b, dims, preferred_element_type=jnp.float32)


def params(mib=24):
    return pltpu.CompilerParams(vmem_limit_bytes=mib * 1024 * 1024)


def shifted(x, by):
    n = lax.axis_size("ctx")
    return lax.ppermute(x, "ctx", [(i, i + by) for i in range(n) if 0 <= i + by < n])


def even_to_odd(x):
    n = lax.axis_size("ctx")
    return lax.ppermute(x, "ctx", [(i, i + 1) for i in range(0, n - 1, 2)])


def odd_to_even(x):
    n = lax.axis_size("ctx")
    return lax.ppermute(x, "ctx", [(i, i - 1) for i in range(1, n, 2)])


def split3(x):
    hi = x.astype(jnp.bfloat16)
    rest = x - hi.astype(jnp.float32)
    mid = rest.astype(jnp.bfloat16)
    low = (rest - mid.astype(jnp.float32)).astype(jnp.bfloat16)
    return hi.astype(jnp.float32), mid.astype(jnp.float32), low.astype(jnp.float32)


def split2(x):
    return split3(x)[:2]


def join2(rows, first):
    return rows[first : first + 1] + rows[first + 1 : first + 2]


def join3(rows, first):
    return rows[first : first + 1] + rows[first + 1 : first + 2] + rows[first + 2 : first + 3]


def stack_rows(rows, count, length):
    spot = lax.broadcasted_iota(jnp.int32, (count, length), 0)
    out = jnp.zeros((count, length), jnp.float32)
    for i, r in enumerate(rows):
        out = jnp.where(spot == i, r, out)
    return out


def softmax_of(parts, scale2):
    top = parts[0]
    for p in parts[1:]:
        top = jnp.maximum(top, p)
    top = jnp.max(top, axis=0, keepdims=True) * scale2
    weights = [jnp.exp2(p * scale2 - top) for p in parts]
    total = weights[0]
    for w in weights[1:]:
        total = total + w
    total = jnp.sum(total, axis=0, keepdims=True)
    return top, total, [w.astype(jnp.bfloat16) for w in weights]


def pick(rows, index):
    spot = lax.broadcasted_iota(jnp.int32, rows.shape, 0)
    return jnp.sum(jnp.where(spot == index, rows, 0.0), axis=0, keepdims=True)


def fetch(pay_ref, k_hbm, v_hbm, source, half, sems, first, at=0):
    length = k_hbm.shape[0]
    copies = []
    for i, hbm in enumerate((k_hbm, v_hbm)):
        lo = at + i * half
        target = pay_ref.at[0:length, lo : lo + half]
        copies.append(pltpu.make_async_copy(hbm.at[:, source : source + half], target, sems.at[first + i]))
        copies[-1].start()
    return copies


def fill(pay_ref, dec, length, dec_row):
    pay_ref[dec_row : dec_row + 16, 0:length] = dec
    if pay_ref.shape[1] > length:
        pay_ref[dec_row : dec_row + 16, length:] = jnp.zeros((16, pay_ref.shape[1] - length), jnp.bfloat16)


def prep_kernel(
    divisor, sizes, docs_ref, mask_ref, ld_ref, k_ref, v_ref,
    thr_ref, start_ref, ahead_ref, entry_ref, keep_ref, cum_ref, cumt_ref, coef_ref, dec_ref, pay_ref, token_ref, sems,
):
    heads, length = ld_ref.shape
    copies = fetch(pay_ref, k_ref, v_ref, 0, sizes[0] * 128, sems, 0)
    tiles = length // BLK
    begin = lax.axis_index("ctx").astype(jnp.int32) * length
    f32, bf16 = jnp.float32, jnp.bfloat16
    parts = jnp.concatenate(split3(ld_ref[...]), axis=0).astype(bf16)
    u = lax.broadcasted_iota(jnp.int32, (length, length), 0)
    t = lax.broadcasted_iota(jnp.int32, (length, length), 1)
    ones = jnp.where(u <= t, 1.0, 0.0).astype(bf16)
    sums = dot(parts, ones, NN)
    cum = sums[:heads] + sums[heads : 2 * heads] + sums[2 * heads :]
    cum_ref[...] = cum
    cumt_ref[...] = jnp.concatenate([cum, jnp.zeros((BLK - heads, length), f32)], axis=0).T
    pos = begin + lax.broadcasted_iota(jnp.int32, (8, length), 1)
    start = jnp.zeros((8, length), jnp.int32)
    ahead = jnp.zeros((8, length), jnp.int32)
    entry = jnp.zeros((8, length), jnp.int32)
    end = jnp.zeros((1, 1), jnp.int32)
    for d in range(docs_ref.shape[1]):
        end = end + docs_ref[:, d : d + 1]
        start = jnp.where(pos >= end, end, start)
        ahead = jnp.where(pos + 2 * length >= end, end, ahead)
        entry = jnp.where(begin - 1 >= end, end, entry)
    start = start - begin
    start_ref[...] = start
    ahead_ref[...] = ahead - (begin + 2 * length)
    entry_ref[...] = entry - begin
    coef_ref[...] = jnp.exp(cum) * jnp.where(start[:1] < 0, 1.0 / divisor, 0.0)
    reach = mask_ref.shape[1]
    tile_row = lax.broadcasted_iota(jnp.int32, (reach, length), 0)
    tile_of = lax.broadcasted_iota(jnp.int32, (reach, length), 1) // BLK
    spread = (lax.broadcasted_iota(jnp.int32, (tiles, length), 1) // BLK == lax.broadcasted_iota(jnp.int32, (tiles, length), 0))
    picked = dot(mask_ref[...].astype(f32).astype(bf16), jnp.where(spread, 1.0, 0.0).astype(bf16), TN)
    keep = (picked > 0.5) | (tile_row == REACH * tiles + tile_of)
    base = (tile_row - REACH * tiles) * BLK
    thr_ref[...] = jnp.where(keep, start[:1] - base, FAR_OFF)
    kept = jnp.where(picked > 0.5, 1.0, 0.0)
    keep_ref[...] = kept[0:16].astype(bf16)
    last = cum[:, length - 1 :]
    first = 0
    for c, n in enumerate(sizes):
        rows = []
        for h in range(first, first + n):
            rows += list(split2(last[h : h + 1] - cum[h : h + 1]))
        for h in range(first, first + n):
            rows += list(split2(last[h : h + 1] + jnp.zeros((1, length), f32)))
        dec = stack_rows(rows, 16, length).astype(bf16)
        dec_ref[c * 16 : (c + 1) * 16, :] = dec
        if c == 0:
            fill(pay_ref, dec, length, length)
        first += n
    token_ref[...] = jnp.zeros_like(token_ref)
    for copy in copies:
        copy.wait()


def pack_kernel(sizes, width1, token_in, q_ref, keep_ref, k_ref, v_ref, dec_ref, one_ref, both_ref, qpay_ref, token_ref, sems):
    length, features = q_ref.shape
    first, second = sizes[0] * 128, (sizes[0] + sizes[1]) * 128
    copies = fetch(one_ref, k_ref, v_ref, first, sizes[1] * 128, sems, 0)
    copies.append(pltpu.make_async_copy(q_ref, qpay_ref.at[0:length, :], sems.at[6]))
    copies[-1].start()
    copies += fetch(both_ref, k_ref, v_ref, first, sizes[1] * 128, sems, 2)
    copies += fetch(both_ref, k_ref, v_ref, second, sizes[2] * 128, sems, 4, width1)
    fill(one_ref, dec_ref[16:32, :], length, length)
    fill(both_ref, dec_ref[16:32, :], length, length)
    fill(both_ref, dec_ref[32:48, :], length, length + 16)
    qpay_ref[length:, 0:length] = keep_ref[...]
    if features > length:
        qpay_ref[length:, length:] = jnp.zeros((16, features - length), jnp.bfloat16)
    token_ref[...] = jnp.zeros_like(token_ref)
    for copy in copies:
        copy.wait()


def pack_last_kernel(sizes, token_in, k_ref, v_ref, dec_ref, pay_ref, token_ref, sems):
    length = k_ref.shape[0]
    copies = fetch(pay_ref, k_ref, v_ref, (sizes[0] + sizes[1]) * 128, sizes[2] * 128, sems, 0)
    fill(pay_ref, dec_ref[...], length, length)
    token_ref[...] = jnp.zeros_like(token_ref)
    for copy in copies:
        copy.wait()


def gate_kernel(token_in, x_in, x_out):
    pass


def own_kernel(scale2, divisor, n, base, q_hbm, k_hbm, v_hbm, thr_ref, start_ref, cum_ref, cumt_ref, o_ref, top_ref, tot_ref, lin_ref, token_ref, held, sems):
    length = q_hbm.shape[0]
    tiles = length // BLK
    own = REACH * tiles
    copies = []
    for i in range(n):
        h = base + i
        for part, hbm in enumerate((q_hbm, k_hbm, v_hbm)):
            source = hbm.at[:, h * 128 : (h + 1) * 128]
            copies.append(pltpu.make_async_copy(source, held.at[3 * i + part], sems.at[3 * i + part]))
            copies[-1].start()
    row = lax.broadcasted_iota(jnp.int32, (BLK, length), 0)
    col = lax.broadcasted_iota(jnp.int32, (BLK, length), 1)
    for i in range(n):
        h = base + i
        for copy in copies[3 * i : 3 * i + 3]:
            copy.wait()
        q, k, v = held[3 * i], held[3 * i + 1], held[3 * i + 2]
        scores = dot(k, q, NT)
        cum_row = cum_ref[h : h + 1, :]
        soft, mix = [], []
        for j in range(tiles):
            s = scores[j * BLK : (j + 1) * BLK]
            causal = row <= col - j * BLK
            soft.append(jnp.where(causal & (row >= thr_ref[own + j : own + j + 1, :]), s, NEG))
            gap = cum_row - cumt_ref[j * BLK : (j + 1) * BLK, h : h + 1]
            ok = causal & (row >= start_ref[0:1, :] - j * BLK)
            decay = jnp.exp(jnp.where(ok, gap, NEG))
            mix.append((s * decay * (1.0 / divisor)).astype(jnp.bfloat16))
        top, total, weights = softmax_of(soft, scale2)
        rows = slice(i * 128, (i + 1) * 128)
        o_ref[rows, :] = dot(v, jnp.concatenate(weights, axis=0), TN)
        lin_ref[rows, :] = dot(v, jnp.concatenate(mix, axis=0), TN)
        top_ref[i : i + 1, :] = top
        tot_ref[i : i + 1, :] = total
    token_ref[...] = jnp.zeros_like(token_ref)


class Pieces:
    def __init__(self, n, two, even, odd, entry, even_at, even_dec):
        self.n, self.two, self.even, self.odd, self.even_at = n, two, even, odd, even_at
        length = self.length = odd.shape[0] - 16
        rows2 = two[length:, 0:length].astype(jnp.float32)
        rows1 = (even[even_dec : even_dec + 16, 0:length] + odd[length:, 0:length]).astype(jnp.float32)
        self.tot1 = [join2(rows1, 2 * n + 2 * i) for i in range(n)]
        self.tot2 = [join2(rows2, 2 * n + 2 * i) for i in range(n)]
        after1 = [join2(rows1, 2 * i) for i in range(n)]
        after2 = [join2(rows2, 2 * i) + self.tot1[i] for i in range(n)]
        col = lax.broadcasted_iota(jnp.int32, (1, length), 1)
        w1 = [jnp.where(col - length >= entry, jnp.exp(x), 0.0) for x in after1]
        w2 = [jnp.where(col - 2 * length >= entry, jnp.exp(x), 0.0) for x in after2]
        self.weight = stack_rows(w1 + w2, BLK, length).T

    def part(self, index):
        cols = slice(index * 128, (index + 1) * 128)
        at = slice(self.even_at + index * 128, self.even_at + (index + 1) * 128)
        return self.two[0 : self.length, cols], self.even[0 : self.length, at] + self.odd[0 : self.length, cols]

    def attend(self, i, q, thr, scale2):
        tiles = self.length // BLK
        k2, k1 = self.part(i)
        v2, v1 = self.part(self.n + i)
        row = lax.broadcasted_iota(jnp.int32, (BLK, q.shape[0]), 0)
        parts = []
        for first, keys in ((0, k2), (tiles, k1)):
            scores = dot(keys, q, NT)
            for j in range(tiles):
                ok = row >= thr[first + j : first + j + 1]
                parts.append(jnp.where(ok, scores[j * BLK : (j + 1) * BLK], NEG))
        top, total, weights = softmax_of(parts, scale2)
        o = dot(v2, jnp.concatenate(weights[:tiles], axis=0), TN) + dot(v1, jnp.concatenate(weights[tiles:], axis=0), TN)
        n = self.n
        kw1 = (k1.astype(jnp.float32) * self.weight[:, i : i + 1]).astype(jnp.bfloat16)
        kw2 = (k2.astype(jnp.float32) * self.weight[:, n + i : n + i + 1]).astype(jnp.bfloat16)
        state = dot(v2, kw2, TN) + dot(v1, kw1, TN)
        return top, total, o, state.astype(jnp.bfloat16)


def far_kernel(scale2, n, even_at, even_dec, token_in, entry_ref, q_ref, keep_ref, ahead_ref, two, even, odd, out_ref, token_ref):
    p = Pieces(n, two, even, odd, entry_ref[0:1, :], even_at, even_dec)
    length = p.length
    keep = keep_ref[...].astype(jnp.float32)
    tiles = length // BLK
    thr = []
    for j in range(2 * tiles):
        base = (j - REACH * tiles) * BLK
        thr.append(jnp.where(keep[j : j + 1] > 0.5, ahead_ref[0:1, :] - base, FAR_OFF))
    thr = jnp.concatenate(thr, axis=0)
    for i in range(n):
        top, total, o, state = p.attend(i, q_ref[0:length, i * 128 : (i + 1) * 128], thr, scale2)
        r = i * 144
        out_ref[r : r + 128, 0:length] = (o * (1.0 / total)).astype(jnp.bfloat16)
        out_ref[r : r + 128, length:] = state
        lse = top + jnp.log(total) * LOG2E
        stats = stack_rows(list(split3(lse)) + [jnp.ones_like(lse)], 16, length)
        out_ref[r + 128 : r + 144, 0:length] = stats.astype(jnp.bfloat16)
        out_ref[r + 128 : r + 144, length:] = jnp.zeros((16, 128), jnp.bfloat16)
    token_ref[...] = jnp.zeros_like(token_ref)


def near_kernel(
    scale2, n, first, even_at, even_dec, token_in, entry_ref, q_ref, thr_ref, coef_ref, two, even, odd, od_ref, topd_ref, totd_ref, lind_ref,
    x_ref, on_ref, st_ref, token_ref,
):
    entry = entry_ref[0:1, :]
    p = Pieces(n, two, even, odd, entry, even_at, even_dec)
    length = p.length
    lses, coefs = [], []
    thr = thr_ref[...]
    for i in range(n):
        q = q_ref[:, i * 128 : (i + 1) * 128]
        rows = slice(i * 128, (i + 1) * 128)
        top, total, o, state = p.attend(i, q, thr, scale2)
        top_d = topd_ref[i : i + 1, :]
        new_top = jnp.maximum(top, top_d)
        a, b = jnp.exp2(top - new_top), jnp.exp2(top_d - new_top)
        total = total * a + totd_ref[i : i + 1, :] * b
        inv = 1.0 / total
        on = o * (a * inv) + od_ref[rows, :] * (b * inv)
        coef = coef_ref[first + i : first + i + 1, :]
        x_ref[rows, :] = lind_ref[rows, :] + dot(state, q, NT) * coef + on
        on_ref[rows, :] = on
        lses.append(new_top + jnp.log(total) * LOG2E)
        through = jnp.where(entry < -2 * length, jnp.exp(p.tot1[i] + p.tot2[i]), 0.0)
        coefs.append(coef * through)
    st_ref[...] = stack_rows(lses + coefs, 8, length)
    token_ref[...] = jnp.zeros_like(token_ref)


def merge_kernel(n, token_in, q_ref, pay_ref, x_ref, on_ref, st_ref, mixed_ref, sq_ref, token_ref):
    squares = None
    length = q_ref.shape[0]
    for i in range(n):
        q = q_ref[:, i * 128 : (i + 1) * 128]
        rows = slice(i * 128, (i + 1) * 128)
        r = i * 144
        stats = pay_ref[r + 128 : r + 144, 0:length].astype(jnp.float32)
        lse_far = join3(stats, 0)
        far = pay_ref[r : r + 128, 0:length].astype(jnp.float32)
        share = 1.0 / (1.0 + jnp.exp2(jnp.minimum(st_ref[i : i + 1, :] - lse_far, 120.0)))
        share = jnp.where((lse_far > 0.5 * NEG) & (stats[3:4] > 0.5), share, 0.0)
        lin = dot(pay_ref[r : r + 128, length:], q, NT) * st_ref[n + i : n + i + 1, :]
        mixed = x_ref[rows, :] + share * (far - on_ref[rows, :]) + lin
        mixed_ref[rows, :] = mixed
        part = jnp.sum(mixed * mixed, axis=0, keepdims=True)
        squares = part if squares is None else squares + part
    sq_ref[...] = squares
    token_ref[...] = jnp.zeros_like(token_ref)


def norm_kernel(parts, *refs):
    mixed_refs, sq_ref, gain_ref, out_ref = refs[:parts], refs[parts], refs[parts + 1], refs[parts + 2]
    inverse = lax.rsqrt(jnp.sum(sq_ref[...], axis=0, keepdims=True) / D + EPSILON)
    col = 0
    for ref in mixed_refs:
        for i in range(ref.shape[0] // 128):
            part = (ref[i * 128 : (i + 1) * 128, :] * inverse).T
            out_ref[:, col : col + 128] = (part * gain_ref[:, col : col + 128]).astype(jnp.bfloat16)
            col += 128


def on_device(query, key, value, log_decay, doc_lengths, tile_mask, gain):
    length, features = query.shape
    heads = log_decay.shape[0]
    hd = features // heads
    tiles = length // BLK
    sizes = [(heads + 2) // 3, (heads + 1) // 3, heads // 3]
    firsts = [sum(sizes[:c]) for c in range(len(sizes))]
    divisor = hd * math.sqrt(length)
    scale2 = LOG2E / math.sqrt(hd)
    f32, bf16 = jnp.float32, jnp.bfloat16
    shape = jax.ShapeDtypeStruct
    loose = pl.BlockSpec(memory_space=pl.ANY)
    hbm = pl.BlockSpec(memory_space=pltpu.HBM)
    dma = pltpu.SemaphoreType.DMA

    def whole(x):
        return pl.BlockSpec(x.shape, lambda *_: (0,) * len(x.shape))

    def cols(c, rows=length):
        return pl.BlockSpec((rows, sizes[c] * hd), lambda *_: (0, firsts[c] // sizes[c]))

    def run(kernel, name, us, specs, args, outs, scratch=()):
        outs = outs + [shape((8, 128), f32)]
        out_specs = [whole(o) for o in outs]
        return pl.pallas_call(
            kernel,
            grid=(1,),
            in_specs=specs,
            out_specs=out_specs,
            out_shape=outs,
            scratch_shapes=scratch,
            compiler_params=params(),
            cost_estimate=pl.CostEstimate(flops=0, bytes_accessed=int(us * 3.69e6), transcendentals=0),
            name=name,
        )(*args)

    def pay_shape(c):
        return shape((length + 16, max(length, 2 * sizes[c] * hd)), bf16)

    docs = doc_lengths[None, :]
    outs = [
        shape(((REACH + 1) * tiles, length), jnp.int32),
        shape((8, length), jnp.int32),
        shape((8, length), jnp.int32),
        shape((8, length), jnp.int32),
        shape((16, length), bf16),
        shape((heads, length), f32),
        shape((length, BLK), f32),
        shape((heads, length), f32),
        shape((16 * len(sizes), length), bf16),
        pay_shape(0),
    ]
    thr, start, ahead, entry, keep, cum, cum_t, coef, dec, pay0, token = run(
        partial(prep_kernel, divisor, sizes),
        "prep",
        2,
        [whole(docs), whole(tile_mask), whole(log_decay), hbm, hbm],
        (docs, tile_mask, log_decay, key, value),
        outs,
        [dma((2,))],
    )
    thr_near = pl.BlockSpec((2 * tiles, length), lambda *_: (1, 0))

    def own(c, token, *after):
        n, first = sizes[c], firsts[c]
        outs = [shape((n * hd, length), f32), shape((n, length), f32), shape((n, length), f32), shape((n * hd, length), f32)]

        def kernel(*refs):
            own_kernel(scale2, divisor, n, first, *refs[len(after) + 1 :])

        *result, token = run(
            kernel,
            "own_piece",
            n * 0.8,
            [loose] * (len(after) + 1) + [hbm] * 3 + [whole(thr), whole(start), whole(cum), whole(cum_t)],
            (*after, token, query, key, value, thr, start, cum, cum_t),
            outs,
            [pltpu.VMEM((3 * n, length, hd), bf16), dma((3 * n,))],
        )
        return result, token

    width1 = pay_shape(1).shape[1]

    def kv(c):
        return two_back[c], from_even[min(c, 1)], from_odd[c]

    def even_place(c):
        return (0, length) if c < 2 else (width1, length + 16)

    def near(c, token):
        n = sizes[c]
        args = (*kv(c), *diag[c])
        x, on, st, token = run(
            partial(near_kernel, scale2, n, firsts[c], *even_place(c)),
            "near_pieces",
            1.8 * n,
            [loose, whole(entry), cols(c), thr_near, whole(coef)] + [whole(a) for a in args],
            (token, entry, query, thr, coef, *args),
            [shape((n * hd, length), f32), shape((n * hd, length), f32), shape((8, length), f32)],
        )
        return (x, on, st), token

    def far(c, token):
        n = sizes[c]
        kept = pl.BlockSpec((16, length), lambda *_: (length // 16, 0))
        pay, token = run(
            partial(far_kernel, scale2, n, *even_place(c)),
            "far_pieces",
            1.5 * n,
            [loose, whole(entry), cols(c), kept, whole(ahead)] + [whole(a) for a in kv(c)],
            (token, entry, q_far, q_far, ahead, *kv(c)),
            [shape((n * (hd + 16), length + hd), bf16)],
        )
        return shifted(pay, 2), token

    def merge(c, token):
        n = sizes[c]
        args = (pays[c], *parts[c])
        return run(
            partial(merge_kernel, n),
            "merge",
            0.5 * n,
            [loose, cols(c)] + [whole(a) for a in args],
            (token, query, *args),
            [shape((n * hd, length), f32), shape((1, length), f32)],
        )

    def gate(x, token):
        return pl.pallas_call(
            gate_kernel,
            in_specs=[loose, loose],
            out_specs=loose,
            out_shape=shape(x.shape, x.dtype),
            input_output_aliases={1: 0},
            compiler_params=params(1),
            name="gate",
        )(token, x)

    chunks = range(len(sizes))
    diag, parts, pays = [None] * 3, [None] * 3, [None] * 3
    two_back, from_even, from_odd = [None] * 3, [None] * 2, [None] * 3
    two_back[0] = shifted(pay0, 2)
    from_even[0] = even_to_odd(pay0)
    diag[0], token = own(0, token)
    one, both, q_pay, token = run(
        partial(pack_kernel, sizes, width1),
        "pack",
        3,
        [loose, hbm, whole(keep), hbm, hbm, whole(dec)],
        (token, query, keep, key, value, dec),
        [pay_shape(1), shape((length + 32, width1 + pay_shape(2).shape[1]), bf16), shape((length + 16, features), bf16)],
        [dma((7,))],
    )
    two_back[1] = shifted(one, 2)
    from_odd[0] = odd_to_even(two_back[0])
    q_far = shifted(q_pay, -2)
    diag[1], token = own(1, token, two_back[0])
    dec_rows = pl.BlockSpec((16, length), lambda *_: (2, 0))
    pay, token = run(
        partial(pack_last_kernel, sizes), "pack", 1, [loose, hbm, hbm, dec_rows], (token, key, value, dec), [pay_shape(2)], [dma((2,))]
    )
    two_back[2] = shifted(pay, 2)
    from_even[1] = even_to_odd(both)
    from_odd[1] = odd_to_even(two_back[1])
    diag[2], token = own(2, token, two_back[1])
    pays[0], token = far(0, token)
    two_back[2] = gate(two_back[2], token)
    from_odd[2] = odd_to_even(two_back[2])
    parts[0], token = near(0, token)
    pays[1], token = far(1, token)
    pays[2], token = far(2, token)
    parts[1], token = near(1, token)
    parts[2], token = near(2, token)
    mixed, total = [], None
    for c in chunks:
        m, s, token = merge(c, token)
        mixed.append(m)
        total = s if total is None else total + s
    ranks = lax.axis_size("head")
    everyone = lax.all_gather(total.reshape(length // 128, 128), "head").reshape(ranks, length)
    gain = gain[None, :]
    return pl.pallas_call(
        partial(norm_kernel, len(mixed)),
        grid=(1,),
        in_specs=[whole(m) for m in mixed] + [whole(everyone), whole(gain)],
        out_specs=whole(query),
        out_shape=shape((length, features), bf16),
        compiler_params=params(),
        name="normalize",
    )(*mixed, everyone, gain)


def solution(mesh):
    placed = (
        P("ctx", "head"),
        P("ctx", "head"),
        P("ctx", "head"),
        P("head", "ctx"),
        P(),
        P("ctx", None),
        P("head"),
    )
    return jax.shard_map(on_device, mesh=mesh, in_specs=placed, out_specs=P("ctx", "head"), check_vma=False)
```

```python
import math
from functools import partial

import jax
import jax.numpy as jnp
from jax import lax
from jax.experimental import pallas as pl
from jax.experimental.pallas import tpu as pltpu
from jax.sharding import PartitionSpec as P

D = 4096
BLK = 128
REACH = 4
EPSILON = 1e-06
NEG = -1e30
FAR_OFF = 1 << 30
LOG2E = math.log2(math.e)

NT = (((1,), (1,)), ((), ()))
TN = (((0,), (0,)), ((), ()))
NN = (((1,), (0,)), ((), ()))


def dot(a, b, dims):
    return lax.dot_general(a, b, dims, preferred_element_type=jnp.float32)


def params(mib=24):
    return pltpu.CompilerParams(vmem_limit_bytes=mib * 1024 * 1024)


def shifted(x, by):
    n = lax.axis_size("ctx")
    return lax.ppermute(x, "ctx", [(i, i + by) for i in range(n) if 0 <= i + by < n])


def even_to_odd(x):
    n = lax.axis_size("ctx")
    return lax.ppermute(x, "ctx", [(i, i + 1) for i in range(0, n - 1, 2)])


def odd_to_even(x):
    n = lax.axis_size("ctx")
    return lax.ppermute(x, "ctx", [(i, i - 1) for i in range(1, n, 2)])


def split3(x):
    hi = x.astype(jnp.bfloat16)
    rest = x - hi.astype(jnp.float32)
    mid = rest.astype(jnp.bfloat16)
    low = (rest - mid.astype(jnp.float32)).astype(jnp.bfloat16)
    return hi.astype(jnp.float32), mid.astype(jnp.float32), low.astype(jnp.float32)


def split2(x):
    return split3(x)[:2]


def join2(rows, first):
    return rows[first : first + 1] + rows[first + 1 : first + 2]


def join3(rows, first):
    return rows[first : first + 1] + rows[first + 1 : first + 2] + rows[first + 2 : first + 3]


def stack_rows(rows, count, length):
    spot = lax.broadcasted_iota(jnp.int32, (count, length), 0)
    out = jnp.zeros((count, length), jnp.float32)
    for i, r in enumerate(rows):
        out = jnp.where(spot == i, r, out)
    return out


def softmax_of(parts, scale2):
    top = parts[0]
    for p in parts[1:]:
        top = jnp.maximum(top, p)
    top = jnp.max(top, axis=0, keepdims=True) * scale2
    weights = [jnp.exp2(p * scale2 - top) for p in parts]
    total = weights[0]
    for w in weights[1:]:
        total = total + w
    total = jnp.sum(total, axis=0, keepdims=True)
    return top, total, [w.astype(jnp.bfloat16) for w in weights]


def pick(rows, index):
    spot = lax.broadcasted_iota(jnp.int32, rows.shape, 0)
    return jnp.sum(jnp.where(spot == index, rows, 0.0), axis=0, keepdims=True)


def fetch(pay_ref, k_hbm, v_hbm, source, half, sems, first, at=0):
    length = k_hbm.shape[0]
    copies = []
    for i, hbm in enumerate((k_hbm, v_hbm)):
        lo = at + i * half
        target = pay_ref.at[0:length, lo : lo + half]
        copies.append(pltpu.make_async_copy(hbm.at[:, source : source + half], target, sems.at[first + i]))
        copies[-1].start()
    return copies


def fill(pay_ref, dec, length, dec_row):
    pay_ref[dec_row : dec_row + 16, 0:length] = dec
    if pay_ref.shape[1] > length:
        pay_ref[dec_row : dec_row + 16, length:] = jnp.zeros((16, pay_ref.shape[1] - length), jnp.bfloat16)


def running_sums(decays):
    heads, length = decays.shape
    parts = jnp.concatenate(split3(decays), axis=0).astype(jnp.bfloat16)
    u = lax.broadcasted_iota(jnp.int32, (length, length), 0)
    t = lax.broadcasted_iota(jnp.int32, (length, length), 1)
    ones = jnp.where(u <= t, 1.0, 0.0).astype(jnp.bfloat16)
    sums = dot(parts, ones, NN)
    return sums[:heads] + sums[heads : 2 * heads] + sums[2 * heads :]


def decay_rows(cum, first, n):
    length = cum.shape[1]
    last = cum[:, length - 1 :]
    rows = []
    for h in range(first, first + n):
        rows += list(split2(last[h : h + 1] - cum[h : h + 1]))
    for h in range(first, first + n):
        rows += list(split2(last[h : h + 1] + jnp.zeros((1, length), jnp.float32)))
    return stack_rows(rows, 16, length).astype(jnp.bfloat16)


def first_kernel(n, ld_ref, k_ref, v_ref, pay_ref, token_ref, sems):
    length = k_ref.shape[0]
    copies = fetch(pay_ref, k_ref, v_ref, 0, n * 128, sems, 0)
    fill(pay_ref, decay_rows(running_sums(ld_ref[...]), 0, n), length, length)
    token_ref[...] = jnp.zeros_like(token_ref)
    for copy in copies:
        copy.wait()


def prep_kernel(
    divisor, sizes, token_in, docs_ref, mask_ref, ld_ref,
    thr_ref, start_ref, ahead_ref, entry_ref, keep_ref, cum_ref, cumt_ref, coef_ref, dec_ref, token_ref,
):
    heads, length = ld_ref.shape
    tiles = length // BLK
    begin = lax.axis_index("ctx").astype(jnp.int32) * length
    f32, bf16 = jnp.float32, jnp.bfloat16
    cum = running_sums(ld_ref[...])
    cum_ref[...] = cum
    cumt_ref[...] = jnp.concatenate([cum, jnp.zeros((BLK - heads, length), f32)], axis=0).T
    pos = begin + lax.broadcasted_iota(jnp.int32, (8, length), 1)
    start = jnp.zeros((8, length), jnp.int32)
    ahead = jnp.zeros((8, length), jnp.int32)
    entry = jnp.zeros((8, length), jnp.int32)
    end = jnp.zeros((1, 1), jnp.int32)
    for d in range(docs_ref.shape[1]):
        end = end + docs_ref[:, d : d + 1]
        start = jnp.where(pos >= end, end, start)
        ahead = jnp.where(pos + 2 * length >= end, end, ahead)
        entry = jnp.where(begin - 1 >= end, end, entry)
    start = start - begin
    start_ref[...] = start
    ahead_ref[...] = ahead - (begin + 2 * length)
    entry_ref[...] = entry - begin
    coef_ref[...] = jnp.exp(cum) * jnp.where(start[:1] < 0, 1.0 / divisor, 0.0)
    reach = mask_ref.shape[1]
    tile_row = lax.broadcasted_iota(jnp.int32, (reach, length), 0)
    tile_of = lax.broadcasted_iota(jnp.int32, (reach, length), 1) // BLK
    spread = (lax.broadcasted_iota(jnp.int32, (tiles, length), 1) // BLK == lax.broadcasted_iota(jnp.int32, (tiles, length), 0))
    picked = dot(mask_ref[...].astype(f32).astype(bf16), jnp.where(spread, 1.0, 0.0).astype(bf16), TN)
    keep = (picked > 0.5) | (tile_row == REACH * tiles + tile_of)
    base = (tile_row - REACH * tiles) * BLK
    thr_ref[...] = jnp.where(keep, start[:1] - base, FAR_OFF)
    kept = jnp.where(picked > 0.5, 1.0, 0.0)
    keep_ref[...] = kept[0:16].astype(bf16)
    first = 0
    for c, n in enumerate(sizes):
        dec_ref[c * 16 : (c + 1) * 16, :] = decay_rows(cum, first, n)
        first += n
    token_ref[...] = jnp.zeros_like(token_ref)


def pack_kernel(sizes, width1, token_in, q_ref, keep_ref, k_ref, v_ref, dec_ref, one_ref, both_ref, qpay_ref, token_ref, sems):
    length, features = q_ref.shape
    first, second = sizes[0] * 128, (sizes[0] + sizes[1]) * 128
    copies = fetch(one_ref, k_ref, v_ref, first, sizes[1] * 128, sems, 0)
    copies.append(pltpu.make_async_copy(q_ref, qpay_ref.at[0:length, :], sems.at[6]))
    copies[-1].start()
    copies += fetch(both_ref, k_ref, v_ref, first, sizes[1] * 128, sems, 2)
    copies += fetch(both_ref, k_ref, v_ref, second, sizes[2] * 128, sems, 4, width1)
    fill(one_ref, dec_ref[16:32, :], length, length)
    fill(both_ref, dec_ref[16:32, :], length, length)
    fill(both_ref, dec_ref[32:48, :], length, length + 16)
    qpay_ref[length:, 0:length] = keep_ref[...]
    if features > length:
        qpay_ref[length:, length:] = jnp.zeros((16, features - length), jnp.bfloat16)
    token_ref[...] = jnp.zeros_like(token_ref)
    for copy in copies:
        copy.wait()


def pack_last_kernel(sizes, token_in, k_ref, v_ref, dec_ref, pay_ref, token_ref, sems):
    length = k_ref.shape[0]
    copies = fetch(pay_ref, k_ref, v_ref, (sizes[0] + sizes[1]) * 128, sizes[2] * 128, sems, 0)
    fill(pay_ref, dec_ref[...], length, length)
    token_ref[...] = jnp.zeros_like(token_ref)
    for copy in copies:
        copy.wait()


def gate_kernel(*refs):
    pass


def own_kernel(scale2, divisor, n, base, q_hbm, k_hbm, v_hbm, thr_ref, start_ref, cum_ref, cumt_ref, o_ref, top_ref, tot_ref, lin_ref, token_ref, held, sems):
    length = q_hbm.shape[0]
    tiles = length // BLK
    own = REACH * tiles
    copies = []
    for i in range(n):
        h = base + i
        for part, hbm in enumerate((q_hbm, k_hbm, v_hbm)):
            source = hbm.at[:, h * 128 : (h + 1) * 128]
            copies.append(pltpu.make_async_copy(source, held.at[3 * i + part], sems.at[3 * i + part]))
            copies[-1].start()
    row = lax.broadcasted_iota(jnp.int32, (BLK, length), 0)
    col = lax.broadcasted_iota(jnp.int32, (BLK, length), 1)
    for i in range(n):
        h = base + i
        for copy in copies[3 * i : 3 * i + 3]:
            copy.wait()
        q, k, v = held[3 * i], held[3 * i + 1], held[3 * i + 2]
        scores = dot(k, q, NT)
        cum_row = cum_ref[h : h + 1, :]
        soft, mix = [], []
        for j in range(tiles):
            s = scores[j * BLK : (j + 1) * BLK]
            causal = row <= col - j * BLK
            soft.append(jnp.where(causal & (row >= thr_ref[own + j : own + j + 1, :]), s, NEG))
            gap = cum_row - cumt_ref[j * BLK : (j + 1) * BLK, h : h + 1]
            ok = causal & (row >= start_ref[0:1, :] - j * BLK)
            decay = jnp.exp(jnp.where(ok, gap, NEG))
            mix.append((s * decay * (1.0 / divisor)).astype(jnp.bfloat16))
        top, total, weights = softmax_of(soft, scale2)
        rows = slice(i * 128, (i + 1) * 128)
        o_ref[rows, :] = dot(v, jnp.concatenate(weights, axis=0), TN)
        lin_ref[rows, :] = dot(v, jnp.concatenate(mix, axis=0), TN)
        top_ref[i : i + 1, :] = top
        tot_ref[i : i + 1, :] = total
    token_ref[...] = jnp.zeros_like(token_ref)


class Pieces:
    def __init__(self, n, two, even, odd, entry, even_at, even_dec):
        self.n, self.two, self.even, self.odd, self.even_at = n, two, even, odd, even_at
        length = self.length = odd.shape[0] - 16
        rows2 = two[length:, 0:length].astype(jnp.float32)
        rows1 = (even[even_dec : even_dec + 16, 0:length] + odd[length:, 0:length]).astype(jnp.float32)
        self.tot1 = [join2(rows1, 2 * n + 2 * i) for i in range(n)]
        self.tot2 = [join2(rows2, 2 * n + 2 * i) for i in range(n)]
        after1 = [join2(rows1, 2 * i) for i in range(n)]
        after2 = [join2(rows2, 2 * i) + self.tot1[i] for i in range(n)]
        col = lax.broadcasted_iota(jnp.int32, (1, length), 1)
        w1 = [jnp.where(col - length >= entry, jnp.exp(x), 0.0) for x in after1]
        w2 = [jnp.where(col - 2 * length >= entry, jnp.exp(x), 0.0) for x in after2]
        self.weight = stack_rows(w1 + w2, BLK, length).T

    def part(self, index):
        cols = slice(index * 128, (index + 1) * 128)
        at = slice(self.even_at + index * 128, self.even_at + (index + 1) * 128)
        return self.two[0 : self.length, cols], self.even[0 : self.length, at] + self.odd[0 : self.length, cols]

    def attend(self, i, q, thr, scale2):
        tiles = self.length // BLK
        k2, k1 = self.part(i)
        v2, v1 = self.part(self.n + i)
        row = lax.broadcasted_iota(jnp.int32, (BLK, q.shape[0]), 0)
        parts = []
        for first, keys in ((0, k2), (tiles, k1)):
            scores = dot(keys, q, NT)
            for j in range(tiles):
                ok = row >= thr[first + j : first + j + 1]
                parts.append(jnp.where(ok, scores[j * BLK : (j + 1) * BLK], NEG))
        top, total, weights = softmax_of(parts, scale2)
        o = dot(v2, jnp.concatenate(weights[:tiles], axis=0), TN) + dot(v1, jnp.concatenate(weights[tiles:], axis=0), TN)
        n = self.n
        kw1 = (k1.astype(jnp.float32) * self.weight[:, i : i + 1]).astype(jnp.bfloat16)
        kw2 = (k2.astype(jnp.float32) * self.weight[:, n + i : n + i + 1]).astype(jnp.bfloat16)
        state = dot(v2, kw2, TN) + dot(v1, kw1, TN)
        return top, total, o, state.astype(jnp.bfloat16)


def far_kernel(scale2, n, even_at, even_dec, token_in, entry_ref, q_ref, keep_ref, ahead_ref, two, even, odd, out_ref, token_ref):
    p = Pieces(n, two, even, odd, entry_ref[0:1, :], even_at, even_dec)
    length = p.length
    keep = keep_ref[...].astype(jnp.float32)
    tiles = length // BLK
    thr = []
    for j in range(2 * tiles):
        base = (j - REACH * tiles) * BLK
        thr.append(jnp.where(keep[j : j + 1] > 0.5, ahead_ref[0:1, :] - base, FAR_OFF))
    thr = jnp.concatenate(thr, axis=0)
    rows = [jnp.ones((1, length), jnp.float32)]
    for i in range(n):
        top, total, o, state = p.attend(i, q_ref[0:length, i * 128 : (i + 1) * 128], thr, scale2)
        r = i * 128
        out_ref[r : r + 128, 0:length] = (o * (1.0 / total)).astype(jnp.bfloat16)
        out_ref[r : r + 128, length:] = state
        lse = top + jnp.log(total) * LOG2E
        rows += list(split3(lse))
    out_ref[n * 128 :, 0:length] = stack_rows(rows, 16, length).astype(jnp.bfloat16)
    out_ref[n * 128 :, length:] = jnp.zeros((16, 128), jnp.bfloat16)
    token_ref[...] = jnp.zeros_like(token_ref)


def near_kernel(
    scale2, n, first, even_at, even_dec, token_in, entry_ref, q_ref, thr_ref, coef_ref, two, even, odd, od_ref, topd_ref, totd_ref, lind_ref,
    x_ref, on_ref, st_ref, token_ref,
):
    entry = entry_ref[0:1, :]
    p = Pieces(n, two, even, odd, entry, even_at, even_dec)
    length = p.length
    lses, coefs = [], []
    thr = thr_ref[...]
    for i in range(n):
        q = q_ref[:, i * 128 : (i + 1) * 128]
        rows = slice(i * 128, (i + 1) * 128)
        top, total, o, state = p.attend(i, q, thr, scale2)
        top_d = topd_ref[i : i + 1, :]
        new_top = jnp.maximum(top, top_d)
        a, b = jnp.exp2(top - new_top), jnp.exp2(top_d - new_top)
        total = total * a + totd_ref[i : i + 1, :] * b
        inv = 1.0 / total
        on = o * (a * inv) + od_ref[rows, :] * (b * inv)
        coef = coef_ref[first + i : first + i + 1, :]
        x_ref[rows, :] = lind_ref[rows, :] + dot(state, q, NT) * coef + on
        on_ref[rows, :] = on
        lses.append(new_top + jnp.log(total) * LOG2E)
        through = jnp.where(entry < -2 * length, jnp.exp(p.tot1[i] + p.tot2[i]), 0.0)
        coefs.append(coef * through)
    st_ref[...] = stack_rows(lses + coefs, 8, length)
    token_ref[...] = jnp.zeros_like(token_ref)


def merge_kernel(n, token_in, q_ref, pay_ref, x_ref, on_ref, st_ref, mixed_ref, sq_ref, token_ref):
    squares = None
    length = q_ref.shape[0]
    stats = pay_ref[n * 128 :, 0:length].astype(jnp.float32)
    for i in range(n):
        q = q_ref[:, i * 128 : (i + 1) * 128]
        rows = slice(i * 128, (i + 1) * 128)
        lse_far = join3(stats, 1 + 3 * i)
        far = pay_ref[rows, 0:length].astype(jnp.float32)
        share = 1.0 / (1.0 + jnp.exp2(jnp.minimum(st_ref[i : i + 1, :] - lse_far, 120.0)))
        share = jnp.where((lse_far > 0.5 * NEG) & (stats[0:1] > 0.5), share, 0.0)
        lin = dot(pay_ref[rows, length:], q, NT) * st_ref[n + i : n + i + 1, :]
        mixed = x_ref[rows, :] + share * (far - on_ref[rows, :]) + lin
        mixed_ref[rows, :] = mixed
        part = jnp.sum(mixed * mixed, axis=0, keepdims=True)
        squares = part if squares is None else squares + part
    sq_ref[...] = squares
    token_ref[...] = jnp.zeros_like(token_ref)


def norm_kernel(parts, *refs):
    mixed_refs, sq_ref, gain_ref, out_ref = refs[:parts], refs[parts], refs[parts + 1], refs[parts + 2]
    inverse = lax.rsqrt(jnp.sum(sq_ref[...], axis=0, keepdims=True) / D + EPSILON)
    col = 0
    for ref in mixed_refs:
        for i in range(ref.shape[0] // 128):
            part = (ref[i * 128 : (i + 1) * 128, :] * inverse).T
            out_ref[:, col : col + 128] = (part * gain_ref[:, col : col + 128]).astype(jnp.bfloat16)
            col += 128


def on_device(query, key, value, log_decay, doc_lengths, tile_mask, gain):
    length, features = query.shape
    heads = log_decay.shape[0]
    hd = features // heads
    tiles = length // BLK
    sizes = [(heads + 2) // 3, (heads + 1) // 3, heads // 3]
    firsts = [sum(sizes[:c]) for c in range(len(sizes))]
    divisor = hd * math.sqrt(length)
    scale2 = LOG2E / math.sqrt(hd)
    f32, bf16 = jnp.float32, jnp.bfloat16
    shape = jax.ShapeDtypeStruct
    loose = pl.BlockSpec(memory_space=pl.ANY)
    hbm = pl.BlockSpec(memory_space=pltpu.HBM)
    dma = pltpu.SemaphoreType.DMA

    def whole(x):
        return pl.BlockSpec(x.shape, lambda *_: (0,) * len(x.shape))

    def cols(c, rows=length):
        return pl.BlockSpec((rows, sizes[c] * hd), lambda *_: (0, firsts[c] // sizes[c]))

    def run(kernel, name, us, specs, args, outs, scratch=(), limit=24):
        outs = outs + [shape((8, 128), f32)]
        out_specs = [whole(o) for o in outs]
        return pl.pallas_call(
            kernel,
            grid=(1,),
            in_specs=specs,
            out_specs=out_specs,
            out_shape=outs,
            scratch_shapes=scratch,
            compiler_params=params(limit),
            cost_estimate=pl.CostEstimate(flops=0, bytes_accessed=int(us * 3.69e6), transcendentals=0),
            name=name,
        )(*args)

    def pay_shape(c):
        return shape((length + 16, max(length, 2 * sizes[c] * hd)), bf16)

    docs = doc_lengths[None, :]
    outs = [
        shape(((REACH + 1) * tiles, length), jnp.int32),
        shape((8, length), jnp.int32),
        shape((8, length), jnp.int32),
        shape((8, length), jnp.int32),
        shape((16, length), bf16),
        shape((heads, length), f32),
        shape((length, BLK), f32),
        shape((heads, length), f32),
        shape((16 * len(sizes), length), bf16),
    ]
    pay0, token = run(
        partial(first_kernel, sizes[0]),
        "first_chunk",
        1,
        [whole(log_decay), hbm, hbm],
        (log_decay, key, value),
        [pay_shape(0)],
        [dma((2,))],
        limit=60,
    )
    thr, start, ahead, entry, keep, cum, cum_t, coef, dec, token = run(
        partial(prep_kernel, divisor, sizes),
        "prep",
        2,
        [loose, whole(docs), whole(tile_mask), whole(log_decay)],
        (token, docs, tile_mask, log_decay),
        outs,
    )
    thr_near = pl.BlockSpec((2 * tiles, length), lambda *_: (1, 0))

    def own(c, token, *after):
        n, first = sizes[c], firsts[c]
        outs = [shape((n * hd, length), f32), shape((n, length), f32), shape((n, length), f32), shape((n * hd, length), f32)]

        def kernel(*refs):
            own_kernel(scale2, divisor, n, first, *refs[len(after) + 1 :])

        *result, token = run(
            kernel,
            "own_piece",
            n * 0.8,
            [loose] * (len(after) + 1) + [hbm] * 3 + [whole(thr), whole(start), whole(cum), whole(cum_t)],
            (*after, token, query, key, value, thr, start, cum, cum_t),
            outs,
            [pltpu.VMEM((3 * n, length, hd), bf16), dma((3 * n,))],
        )
        return result, token

    width1 = pay_shape(1).shape[1]

    def kv(c):
        return two_back[c], from_even[min(c, 1)], from_odd[c]

    def even_place(c):
        return (0, length) if c < 2 else (width1, length + 16)

    def near(c, token):
        n = sizes[c]
        args = (*kv(c), *diag[c])
        x, on, st, token = run(
            partial(near_kernel, scale2, n, firsts[c], *even_place(c)),
            "near_pieces",
            1.8 * n,
            [loose, whole(entry), cols(c), thr_near, whole(coef)] + [whole(a) for a in args],
            (token, entry, query, thr, coef, *args),
            [shape((n * hd, length), f32), shape((n * hd, length), f32), shape((8, length), f32)],
        )
        return (x, on, st), token

    def far(c, token):
        n = sizes[c]
        kept = pl.BlockSpec((16, length), lambda *_: (length // 16, 0))
        pay, token = run(
            partial(far_kernel, scale2, n, *even_place(c)),
            "far_pieces",
            1.5 * n,
            [loose, whole(entry), cols(c), kept, whole(ahead)] + [whole(a) for a in kv(c)],
            (token, entry, q_far, q_far, ahead, *kv(c)),
            [shape((n * hd + 16, length + hd), bf16)],
        )
        return shifted(pay, 2), token

    def merge(c, token):
        n = sizes[c]
        args = (pays[c], *parts[c])
        return run(
            partial(merge_kernel, n),
            "merge",
            0.5 * n,
            [loose, cols(c)] + [whole(a) for a in args],
            (token, query, *args),
            [shape((n * hd, length), f32), shape((1, length), f32)],
        )

    def gate(x, *after):
        return pl.pallas_call(
            gate_kernel,
            in_specs=[loose] * (1 + len(after)),
            out_specs=loose,
            out_shape=shape(x.shape, x.dtype),
            input_output_aliases={0: 0},
            compiler_params=params(1),
            name="gate",
        )(x, *after)

    chunks = range(len(sizes))
    diag, parts, pays = [None] * 3, [None] * 3, [None] * 3
    two_back, from_even, from_odd = [None] * 3, [None] * 2, [None] * 3
    two_back[0] = shifted(pay0, 2)
    from_even[0] = even_to_odd(pay0)
    diag[0], token = own(0, token)
    one, both, q_pay, token = run(
        partial(pack_kernel, sizes, width1),
        "pack",
        3,
        [loose, hbm, whole(keep), hbm, hbm, whole(dec)],
        (token, query, keep, key, value, dec),
        [pay_shape(1), shape((length + 32, width1 + pay_shape(2).shape[1]), bf16), shape((length + 16, features), bf16)],
        [dma((7,))],
    )
    two_back[1] = shifted(one, 2)
    from_odd[0] = odd_to_even(two_back[0])
    q_far = shifted(q_pay, -2)
    diag[1], token = own(1, token, two_back[0])
    dec_rows = pl.BlockSpec((16, length), lambda *_: (2, 0))
    pay, token = run(
        partial(pack_last_kernel, sizes), "pack", 1, [loose, hbm, hbm, dec_rows], (token, key, value, dec), [pay_shape(2)], [dma((2,))]
    )
    two_back[2] = shifted(pay, 2)
    from_even[1] = even_to_odd(both)
    from_odd[1] = odd_to_even(two_back[1])
    diag[2], token = own(2, token)
    pays[0], token = far(0, token)
    parts[0], token = near(0, token)
    two_back[2] = gate(two_back[2], token)
    from_odd[2] = odd_to_even(two_back[2])
    pays[1], token = far(1, token)
    parts[1], token = near(1, token)
    pays[2], token = far(2, token)
    parts[2], token = near(2, token)
    mixed, total = [], None
    for c in chunks:
        m, s, token = merge(c, token)
        mixed.append(m)
        total = s if total is None else total + s
    ranks = lax.axis_size("head")
    everyone = lax.all_gather(total.reshape(length // 128, 128), "head").reshape(ranks, length)
    gain = gain[None, :]
    return pl.pallas_call(
        partial(norm_kernel, len(mixed)),
        grid=(1,),
        in_specs=[whole(m) for m in mixed] + [whole(everyone), whole(gain)],
        out_specs=whole(query),
        out_shape=shape((length, features), bf16),
        compiler_params=params(),
        name="normalize",
    )(*mixed, everyone, gain)


def solution(mesh):
    placed = (
        P("ctx", "head"),
        P("ctx", "head"),
        P("ctx", "head"),
        P("head", "ctx"),
        P(),
        P("ctx", None),
        P("head"),
    )
    return jax.shard_map(on_device, mesh=mesh, in_specs=placed, out_specs=P("ctx", "head"), check_vma=False)
```

```python
import math
from functools import partial

import jax
import jax.numpy as jnp
from jax import lax
from jax.experimental import pallas as pl
from jax.experimental.pallas import tpu as pltpu
from jax.sharding import PartitionSpec as P

D = 4096
BLK = 128
REACH = 4
EPSILON = 1e-06
NEG = -1e30
FAR_OFF = 1 << 30
LOG2E = math.log2(math.e)

NT = (((1,), (1,)), ((), ()))
TN = (((0,), (0,)), ((), ()))
NN = (((1,), (0,)), ((), ()))


def dot(a, b, dims):
    return lax.dot_general(a, b, dims, preferred_element_type=jnp.float32)


def params(mib=24):
    return pltpu.CompilerParams(vmem_limit_bytes=mib * 1024 * 1024)


def shifted(x, by):
    n = lax.axis_size("ctx")
    return lax.ppermute(x, "ctx", [(i, i + by) for i in range(n) if 0 <= i + by < n])


def even_to_odd(x):
    n = lax.axis_size("ctx")
    return lax.ppermute(x, "ctx", [(i, i + 1) for i in range(0, n - 1, 2)])


def odd_to_even(x):
    n = lax.axis_size("ctx")
    return lax.ppermute(x, "ctx", [(i, i - 1) for i in range(1, n, 2)])


def split3(x):
    hi = x.astype(jnp.bfloat16)
    rest = x - hi.astype(jnp.float32)
    mid = rest.astype(jnp.bfloat16)
    low = (rest - mid.astype(jnp.float32)).astype(jnp.bfloat16)
    return hi.astype(jnp.float32), mid.astype(jnp.float32), low.astype(jnp.float32)


def split2(x):
    return split3(x)[:2]


def join2(rows, first):
    return rows[first : first + 1] + rows[first + 1 : first + 2]


def join3(rows, first):
    return rows[first : first + 1] + rows[first + 1 : first + 2] + rows[first + 2 : first + 3]


def stack_rows(rows, count, length):
    spot = lax.broadcasted_iota(jnp.int32, (count, length), 0)
    out = jnp.zeros((count, length), jnp.float32)
    for i, r in enumerate(rows):
        out = jnp.where(spot == i, r, out)
    return out


def softmax_of(parts, scale2):
    top = parts[0]
    for p in parts[1:]:
        top = jnp.maximum(top, p)
    top = jnp.max(top, axis=0, keepdims=True) * scale2
    weights = [jnp.exp2(p * scale2 - top) for p in parts]
    total = weights[0]
    for w in weights[1:]:
        total = total + w
    total = jnp.sum(total, axis=0, keepdims=True)
    return top, total, [w.astype(jnp.bfloat16) for w in weights]


def pick(rows, index):
    spot = lax.broadcasted_iota(jnp.int32, rows.shape, 0)
    return jnp.sum(jnp.where(spot == index, rows, 0.0), axis=0, keepdims=True)


def fetch(pay_ref, k_hbm, v_hbm, source, half, sems, first, at=0):
    length = k_hbm.shape[0]
    copies = []
    for i, hbm in enumerate((k_hbm, v_hbm)):
        lo = at + i * half
        target = pay_ref.at[0:length, lo : lo + half]
        copies.append(pltpu.make_async_copy(hbm.at[:, source : source + half], target, sems.at[first + i]))
        copies[-1].start()
    return copies


def fill(pay_ref, dec, length, dec_row):
    pay_ref[dec_row : dec_row + 16, 0:length] = dec
    if pay_ref.shape[1] > length:
        pay_ref[dec_row : dec_row + 16, length:] = jnp.zeros((16, pay_ref.shape[1] - length), jnp.bfloat16)


def running_sums(decays):
    heads, length = decays.shape
    parts = jnp.concatenate(split3(decays), axis=0).astype(jnp.bfloat16)
    u = lax.broadcasted_iota(jnp.int32, (length, length), 0)
    t = lax.broadcasted_iota(jnp.int32, (length, length), 1)
    ones = jnp.where(u <= t, 1.0, 0.0).astype(jnp.bfloat16)
    sums = dot(parts, ones, NN)
    return sums[:heads] + sums[heads : 2 * heads] + sums[2 * heads :]


def decay_rows(cum, first, n):
    length = cum.shape[1]
    last = cum[:, length - 1 :]
    rows = []
    for h in range(first, first + n):
        rows += list(split2(last[h : h + 1] - cum[h : h + 1]))
    for h in range(first, first + n):
        rows += list(split2(last[h : h + 1] + jnp.zeros((1, length), jnp.float32)))
    return stack_rows(rows, 16, length).astype(jnp.bfloat16)


def first_kernel(n, ld_hbm, k_hbm, v_hbm, pay_hbm, token_ref, ld_ref, stage_ref, sems):
    length = k_hbm.shape[0]
    half = n * 128
    decays = pltpu.make_async_copy(ld_hbm, ld_ref, sems.at[0])
    decays.start()
    loads = fetch(stage_ref, k_hbm, v_hbm, 0, half, sems, 1)
    decays.wait()
    fill(stage_ref, decay_rows(running_sums(ld_ref[...]), 0, n), length, length)
    stores = [pltpu.make_async_copy(stage_ref.at[length : length + 16, :], pay_hbm.at[length : length + 16, :], sems.at[3])]
    stores[-1].start()
    for i in range(2):
        loads[i].wait()
        where = (slice(0, length), slice(i * half, (i + 1) * half))
        stores.append(pltpu.make_async_copy(stage_ref.at[where], pay_hbm.at[where], sems.at[4 + i]))
        stores[-1].start()
    token_ref[...] = jnp.zeros_like(token_ref)
    for store in stores:
        store.wait()


def prep_kernel(
    divisor, sizes, token_in, docs_ref, mask_ref, ld_ref,
    thr_ref, start_ref, ahead_ref, entry_ref, keep_ref, cum_ref, cumt_ref, coef_ref, dec_ref, token_ref,
):
    heads, length = ld_ref.shape
    tiles = length // BLK
    begin = lax.axis_index("ctx").astype(jnp.int32) * length
    f32, bf16 = jnp.float32, jnp.bfloat16
    cum = running_sums(ld_ref[...])
    cum_ref[...] = cum
    cumt_ref[...] = jnp.concatenate([cum, jnp.zeros((BLK - heads, length), f32)], axis=0).T
    pos = begin + lax.broadcasted_iota(jnp.int32, (8, length), 1)
    start = jnp.zeros((8, length), jnp.int32)
    ahead = jnp.zeros((8, length), jnp.int32)
    entry = jnp.zeros((8, length), jnp.int32)
    end = jnp.zeros((1, 1), jnp.int32)
    for d in range(docs_ref.shape[1]):
        end = end + docs_ref[:, d : d + 1]
        start = jnp.where(pos >= end, end, start)
        ahead = jnp.where(pos + 2 * length >= end, end, ahead)
        entry = jnp.where(begin - 1 >= end, end, entry)
    start = start - begin
    start_ref[...] = start
    ahead_ref[...] = ahead - (begin + 2 * length)
    entry_ref[...] = entry - begin
    coef_ref[...] = jnp.exp(cum) * jnp.where(start[:1] < 0, 1.0 / divisor, 0.0)
    reach = mask_ref.shape[1]
    tile_row = lax.broadcasted_iota(jnp.int32, (reach, length), 0)
    tile_of = lax.broadcasted_iota(jnp.int32, (reach, length), 1) // BLK
    spread = (lax.broadcasted_iota(jnp.int32, (tiles, length), 1) // BLK == lax.broadcasted_iota(jnp.int32, (tiles, length), 0))
    picked = dot(mask_ref[...].astype(f32).astype(bf16), jnp.where(spread, 1.0, 0.0).astype(bf16), TN)
    keep = (picked > 0.5) | (tile_row == REACH * tiles + tile_of)
    base = (tile_row - REACH * tiles) * BLK
    thr_ref[...] = jnp.where(keep, start[:1] - base, FAR_OFF)
    kept = jnp.where(picked > 0.5, 1.0, 0.0)
    keep_ref[...] = kept[0:16].astype(bf16)
    first = 0
    for c, n in enumerate(sizes):
        dec_ref[c * 16 : (c + 1) * 16, :] = decay_rows(cum, first, n)
        first += n
    token_ref[...] = jnp.zeros_like(token_ref)


def pack_kernel(sizes, width1, token_in, q_ref, keep_ref, k_ref, v_ref, dec_ref, one_ref, both_ref, qpay_ref, token_ref, sems):
    length, features = q_ref.shape
    first, second = sizes[0] * 128, (sizes[0] + sizes[1]) * 128
    copies = fetch(one_ref, k_ref, v_ref, first, sizes[1] * 128, sems, 0)
    copies.append(pltpu.make_async_copy(q_ref, qpay_ref.at[0:length, :], sems.at[6]))
    copies[-1].start()
    copies += fetch(both_ref, k_ref, v_ref, first, sizes[1] * 128, sems, 2)
    copies += fetch(both_ref, k_ref, v_ref, second, sizes[2] * 128, sems, 4, width1)
    fill(one_ref, dec_ref[16:32, :], length, length)
    fill(both_ref, dec_ref[16:32, :], length, length)
    fill(both_ref, dec_ref[32:48, :], length, length + 16)
    qpay_ref[length:, 0:length] = keep_ref[...]
    if features > length:
        qpay_ref[length:, length:] = jnp.zeros((16, features - length), jnp.bfloat16)
    token_ref[...] = jnp.zeros_like(token_ref)
    for copy in copies:
        copy.wait()


def pack_last_kernel(sizes, token_in, k_ref, v_ref, dec_ref, pay_ref, token_ref, sems):
    length = k_ref.shape[0]
    copies = fetch(pay_ref, k_ref, v_ref, (sizes[0] + sizes[1]) * 128, sizes[2] * 128, sems, 0)
    fill(pay_ref, dec_ref[...], length, length)
    token_ref[...] = jnp.zeros_like(token_ref)
    for copy in copies:
        copy.wait()


def gate_kernel(*refs):
    pass


def own_kernel(scale2, divisor, n, base, q_hbm, k_hbm, v_hbm, thr_ref, start_ref, cum_ref, cumt_ref, o_ref, top_ref, tot_ref, lin_ref, token_ref, held, sems):
    length = q_hbm.shape[0]
    tiles = length // BLK
    own = REACH * tiles
    copies = []
    for i in range(n):
        h = base + i
        for part, hbm in enumerate((q_hbm, k_hbm, v_hbm)):
            source = hbm.at[:, h * 128 : (h + 1) * 128]
            copies.append(pltpu.make_async_copy(source, held.at[3 * i + part], sems.at[3 * i + part]))
            copies[-1].start()
    row = lax.broadcasted_iota(jnp.int32, (BLK, length), 0)
    col = lax.broadcasted_iota(jnp.int32, (BLK, length), 1)
    for i in range(n):
        h = base + i
        for copy in copies[3 * i : 3 * i + 3]:
            copy.wait()
        q, k, v = held[3 * i], held[3 * i + 1], held[3 * i + 2]
        scores = dot(k, q, NT)
        cum_row = cum_ref[h : h + 1, :]
        soft, mix = [], []
        for j in range(tiles):
            s = scores[j * BLK : (j + 1) * BLK]
            causal = row <= col - j * BLK
            soft.append(jnp.where(causal & (row >= thr_ref[own + j : own + j + 1, :]), s, NEG))
            gap = cum_row - cumt_ref[j * BLK : (j + 1) * BLK, h : h + 1]
            ok = causal & (row >= start_ref[0:1, :] - j * BLK)
            decay = jnp.exp(jnp.where(ok, gap, NEG))
            mix.append((s * decay * (1.0 / divisor)).astype(jnp.bfloat16))
        top, total, weights = softmax_of(soft, scale2)
        rows = slice(i * 128, (i + 1) * 128)
        o_ref[rows, :] = dot(v, jnp.concatenate(weights, axis=0), TN)
        lin_ref[rows, :] = dot(v, jnp.concatenate(mix, axis=0), TN)
        top_ref[i : i + 1, :] = top
        tot_ref[i : i + 1, :] = total
    token_ref[...] = jnp.zeros_like(token_ref)


def partial_softmax(q, groups, thr, scale2):
    tiles = groups[0][1].shape[0] // BLK
    row = lax.broadcasted_iota(jnp.int32, (BLK, q.shape[0]), 0)
    parts = []
    for first, keys, _ in groups:
        scores = dot(keys, q, NT)
        for j in range(tiles):
            ok = row >= thr[first + j : first + j + 1]
            parts.append(jnp.where(ok, scores[j * BLK : (j + 1) * BLK], NEG))
    top, total, weights = softmax_of(parts, scale2)
    o = None
    for g, (_, _, values) in enumerate(groups):
        here = dot(values, jnp.concatenate(weights[g * tiles : (g + 1) * tiles], axis=0), TN)
        o = here if o is None else o + here
    return top, total, o


def earlier_kernel(scale2, n, token_in, q_ref, thr_ref, two, od_ref, topd_ref, totd_ref, o_ref, top_ref, tot_ref, token_ref):
    length = q_ref.shape[0]
    thr = thr_ref[...]
    for i in range(n):
        rows = slice(i * 128, (i + 1) * 128)
        keys = two[0:length, i * 128 : (i + 1) * 128]
        values = two[0:length, (n + i) * 128 : (n + i + 1) * 128]
        top, total, o = partial_softmax(q_ref[:, rows], [(0, keys, values)], thr, scale2)
        top_d = topd_ref[i : i + 1, :]
        new_top = jnp.maximum(top, top_d)
        a, b = jnp.exp2(top - new_top), jnp.exp2(top_d - new_top)
        o_ref[rows, :] = o * a + od_ref[rows, :] * b
        top_ref[i : i + 1, :] = new_top
        tot_ref[i : i + 1, :] = total * a + totd_ref[i : i + 1, :] * b
    token_ref[...] = jnp.zeros_like(token_ref)


class Pieces:
    def __init__(self, n, two, even, odd, entry, even_at, even_dec):
        self.n, self.two, self.even, self.odd, self.even_at = n, two, even, odd, even_at
        length = self.length = odd.shape[0] - 16
        rows2 = two[length:, 0:length].astype(jnp.float32)
        rows1 = (even[even_dec : even_dec + 16, 0:length] + odd[length:, 0:length]).astype(jnp.float32)
        self.tot1 = [join2(rows1, 2 * n + 2 * i) for i in range(n)]
        self.tot2 = [join2(rows2, 2 * n + 2 * i) for i in range(n)]
        after1 = [join2(rows1, 2 * i) for i in range(n)]
        after2 = [join2(rows2, 2 * i) + self.tot1[i] for i in range(n)]
        col = lax.broadcasted_iota(jnp.int32, (1, length), 1)
        w1 = [jnp.where(col - length >= entry, jnp.exp(x), 0.0) for x in after1]
        w2 = [jnp.where(col - 2 * length >= entry, jnp.exp(x), 0.0) for x in after2]
        self.weight = stack_rows(w1 + w2, BLK, length).T

    def part(self, index):
        cols = slice(index * 128, (index + 1) * 128)
        at = slice(self.even_at + index * 128, self.even_at + (index + 1) * 128)
        return self.two[0 : self.length, cols], self.even[0 : self.length, at] + self.odd[0 : self.length, cols]

    def attend(self, i, q, thr, scale2, both=True):
        tiles = self.length // BLK
        k2, k1 = self.part(i)
        v2, v1 = self.part(self.n + i)
        groups = [(0, k2, v2), (tiles, k1, v1)] if both else [(tiles, k1, v1)]
        top, total, o = partial_softmax(q, groups, thr, scale2)
        n = self.n
        kw1 = (k1.astype(jnp.float32) * self.weight[:, i : i + 1]).astype(jnp.bfloat16)
        kw2 = (k2.astype(jnp.float32) * self.weight[:, n + i : n + i + 1]).astype(jnp.bfloat16)
        state = dot(v2, kw2, TN) + dot(v1, kw1, TN)
        return top, total, o, state.astype(jnp.bfloat16)


def far_thresholds(keep_ref, ahead_ref):
    keep = keep_ref[...].astype(jnp.float32)
    tiles = keep.shape[1] // BLK
    thr = []
    for j in range(2 * tiles):
        base = (j - REACH * tiles) * BLK
        thr.append(jnp.where(keep[j : j + 1] > 0.5, ahead_ref[0:1, :] - base, FAR_OFF))
    return jnp.concatenate(thr, axis=0)


def far_earlier_kernel(scale2, n, token_in, q_ref, keep_ref, ahead_ref, two, o_ref, top_ref, tot_ref, token_ref):
    thr = far_thresholds(keep_ref, ahead_ref)
    length = thr.shape[1]
    for i in range(n):
        rows = slice(i * 128, (i + 1) * 128)
        keys = two[0:length, i * 128 : (i + 1) * 128]
        values = two[0:length, (n + i) * 128 : (n + i + 1) * 128]
        top, total, o = partial_softmax(q_ref[0:length, rows], [(0, keys, values)], thr, scale2)
        o_ref[rows, :] = o
        top_ref[i : i + 1, :] = top
        tot_ref[i : i + 1, :] = total
    token_ref[...] = jnp.zeros_like(token_ref)


def far_kernel(scale2, n, both, even_at, even_dec, token_in, entry_ref, q_ref, keep_ref, ahead_ref, two, even, odd, *rest):
    out_ref, token_ref = rest[-2:]
    p = Pieces(n, two, even, odd, entry_ref[0:1, :], even_at, even_dec)
    length = p.length
    thr = far_thresholds(keep_ref, ahead_ref)
    rows = [jnp.ones((1, length), jnp.float32)]
    for i in range(n):
        top, total, o, state = p.attend(i, q_ref[0:length, i * 128 : (i + 1) * 128], thr, scale2, both)
        if not both:
            o_e, top_e, tot_e = rest[0][i * 128 : (i + 1) * 128, :], rest[1][i : i + 1, :], rest[2][i : i + 1, :]
            new_top = jnp.maximum(top, top_e)
            a, b = jnp.exp2(top - new_top), jnp.exp2(top_e - new_top)
            top, total, o = new_top, total * a + tot_e * b, o * a + o_e * b
        r = i * 128
        out_ref[r : r + 128, 0:length] = (o * (1.0 / total)).astype(jnp.bfloat16)
        out_ref[r : r + 128, length:] = state
        lse = top + jnp.log(total) * LOG2E
        rows += list(split3(lse))
    out_ref[n * 128 :, 0:length] = stack_rows(rows, 16, length).astype(jnp.bfloat16)
    out_ref[n * 128 :, length:] = jnp.zeros((16, 128), jnp.bfloat16)
    token_ref[...] = jnp.zeros_like(token_ref)


def near_kernel(
    scale2, n, first, both, even_at, even_dec, token_in, entry_ref, q_ref, thr_ref, coef_ref, two, even, odd, od_ref, topd_ref, totd_ref, lind_ref,
    x_ref, on_ref, st_ref, token_ref,
):
    entry = entry_ref[0:1, :]
    p = Pieces(n, two, even, odd, entry, even_at, even_dec)
    length = p.length
    lses, coefs = [], []
    thr = thr_ref[...]
    for i in range(n):
        q = q_ref[:, i * 128 : (i + 1) * 128]
        rows = slice(i * 128, (i + 1) * 128)
        top, total, o, state = p.attend(i, q, thr, scale2, both)
        top_d = topd_ref[i : i + 1, :]
        new_top = jnp.maximum(top, top_d)
        a, b = jnp.exp2(top - new_top), jnp.exp2(top_d - new_top)
        total = total * a + totd_ref[i : i + 1, :] * b
        inv = 1.0 / total
        on = o * (a * inv) + od_ref[rows, :] * (b * inv)
        coef = coef_ref[first + i : first + i + 1, :]
        x_ref[rows, :] = lind_ref[rows, :] + dot(state, q, NT) * coef + on
        on_ref[rows, :] = on
        lses.append(new_top + jnp.log(total) * LOG2E)
        through = jnp.where(entry < -2 * length, jnp.exp(p.tot1[i] + p.tot2[i]), 0.0)
        coefs.append(coef * through)
    st_ref[...] = stack_rows(lses + coefs, 8, length)
    token_ref[...] = jnp.zeros_like(token_ref)


def merge_kernel(n, token_in, q_ref, pay_ref, x_ref, on_ref, st_ref, mixed_ref, sq_ref, token_ref):
    squares = None
    length = q_ref.shape[0]
    stats = pay_ref[n * 128 :, 0:length].astype(jnp.float32)
    for i in range(n):
        q = q_ref[:, i * 128 : (i + 1) * 128]
        rows = slice(i * 128, (i + 1) * 128)
        lse_far = join3(stats, 1 + 3 * i)
        far = pay_ref[rows, 0:length].astype(jnp.float32)
        share = 1.0 / (1.0 + jnp.exp2(jnp.minimum(st_ref[i : i + 1, :] - lse_far, 120.0)))
        share = jnp.where((lse_far > 0.5 * NEG) & (stats[0:1] > 0.5), share, 0.0)
        lin = dot(pay_ref[rows, length:], q, NT) * st_ref[n + i : n + i + 1, :]
        mixed = x_ref[rows, :] + share * (far - on_ref[rows, :]) + lin
        mixed_ref[rows, :] = mixed
        part = jnp.sum(mixed * mixed, axis=0, keepdims=True)
        squares = part if squares is None else squares + part
    sq_ref[...] = squares
    token_ref[...] = jnp.zeros_like(token_ref)


def norm_kernel(parts, *refs):
    mixed_refs, sq_ref, gain_ref, out_ref = refs[:parts], refs[parts], refs[parts + 1], refs[parts + 2]
    inverse = lax.rsqrt(jnp.sum(sq_ref[...], axis=0, keepdims=True) / D + EPSILON)
    col = 0
    for ref in mixed_refs:
        for i in range(ref.shape[0] // 128):
            part = (ref[i * 128 : (i + 1) * 128, :] * inverse).T
            out_ref[:, col : col + 128] = (part * gain_ref[:, col : col + 128]).astype(jnp.bfloat16)
            col += 128


def on_device(query, key, value, log_decay, doc_lengths, tile_mask, gain):
    length, features = query.shape
    heads = log_decay.shape[0]
    hd = features // heads
    tiles = length // BLK
    sizes = [(heads + 2) // 3, (heads + 1) // 3, heads // 3]
    firsts = [sum(sizes[:c]) for c in range(len(sizes))]
    divisor = hd * math.sqrt(length)
    scale2 = LOG2E / math.sqrt(hd)
    f32, bf16 = jnp.float32, jnp.bfloat16
    shape = jax.ShapeDtypeStruct
    loose = pl.BlockSpec(memory_space=pl.ANY)
    hbm = pl.BlockSpec(memory_space=pltpu.HBM)
    dma = pltpu.SemaphoreType.DMA

    def whole(x):
        return pl.BlockSpec(x.shape, lambda *_: (0,) * len(x.shape))

    def cols(c, rows=length):
        return pl.BlockSpec((rows, sizes[c] * hd), lambda *_: (0, firsts[c] // sizes[c]))

    def run(kernel, name, us, specs, args, outs, scratch=(), limit=24, out_specs=None):
        outs = outs + [shape((8, 128), f32)]
        out_specs = (out_specs or [whole(o) for o in outs[:-1]]) + [whole(outs[-1])]
        return pl.pallas_call(
            kernel,
            grid=(1,),
            in_specs=specs,
            out_specs=out_specs,
            out_shape=outs,
            scratch_shapes=scratch,
            compiler_params=params(limit),
            cost_estimate=pl.CostEstimate(flops=0, bytes_accessed=int(us * 3.69e6), transcendentals=0),
            name=name,
        )(*args)

    def pay_shape(c):
        return shape((length + 16, max(length, 2 * sizes[c] * hd)), bf16)

    docs = doc_lengths[None, :]
    outs = [
        shape(((REACH + 1) * tiles, length), jnp.int32),
        shape((8, length), jnp.int32),
        shape((8, length), jnp.int32),
        shape((8, length), jnp.int32),
        shape((16, length), bf16),
        shape((heads, length), f32),
        shape((length, BLK), f32),
        shape((heads, length), f32),
        shape((16 * len(sizes), length), bf16),
    ]
    pay0, token = run(
        partial(first_kernel, sizes[0]),
        "first_chunk",
        1,
        [hbm, hbm, hbm],
        (log_decay, key, value),
        [pay_shape(0)],
        [pltpu.VMEM(log_decay.shape, f32), pltpu.VMEM(pay_shape(0).shape, bf16), dma((6,))],
        limit=60,
        out_specs=[hbm],
    )
    thr, start, ahead, entry, keep, cum, cum_t, coef, dec, token = run(
        partial(prep_kernel, divisor, sizes),
        "prep",
        2,
        [loose, whole(docs), whole(tile_mask), whole(log_decay)],
        (token, docs, tile_mask, log_decay),
        outs,
    )
    thr_near = pl.BlockSpec((2 * tiles, length), lambda *_: (1, 0))

    def own(c, token, *after):
        n, first = sizes[c], firsts[c]
        outs = [shape((n * hd, length), f32), shape((n, length), f32), shape((n, length), f32), shape((n * hd, length), f32)]

        def kernel(*refs):
            own_kernel(scale2, divisor, n, first, *refs[len(after) + 1 :])

        *result, token = run(
            kernel,
            "own_piece",
            n * 0.8,
            [loose] * (len(after) + 1) + [hbm] * 3 + [whole(thr), whole(start), whole(cum), whole(cum_t)],
            (*after, token, query, key, value, thr, start, cum, cum_t),
            outs,
            [pltpu.VMEM((3 * n, length, hd), bf16), dma((3 * n,))],
        )
        return result, token

    width1 = pay_shape(1).shape[1]

    def kv(c):
        return two_back[c], from_even[min(c, 1)], from_odd[c]

    def even_place(c):
        return (0, length) if c < 2 else (width1, length + 16)

    def near(c, token):
        n = sizes[c]
        args = (*kv(c), *diag[c])
        x, on, st, token = run(
            partial(near_kernel, scale2, n, firsts[c], c != 1, *even_place(c)),
            "near_pieces",
            1.8 * n,
            [loose, whole(entry), cols(c), thr_near, whole(coef)] + [whole(a) for a in args],
            (token, entry, query, thr, coef, *args),
            [shape((n * hd, length), f32), shape((n * hd, length), f32), shape((8, length), f32)],
        )
        return (x, on, st), token

    def earlier(c, token):
        n = sizes[c]
        args = (two_back[c], *diag[c][:3])
        o, top, tot, token = run(
            partial(earlier_kernel, scale2, n),
            "earlier_piece",
            0.8 * n,
            [loose, cols(c), thr_near] + [whole(a) for a in args],
            (token, query, thr, *args),
            [shape((n * hd, length), f32), shape((n, length), f32), shape((n, length), f32)],
        )
        diag[c] = [o, top, tot, diag[c][3]]
        return token

    kept = pl.BlockSpec((16, length), lambda *_: (length // 16, 0))

    def far_earlier(c, token):
        n = sizes[c]
        *first, token = run(
            partial(far_earlier_kernel, scale2, n),
            "far_earlier",
            0.7 * n,
            [loose, cols(c), kept, whole(ahead), whole(two_back[c])],
            (token, q_far, q_far, ahead, two_back[c]),
            [shape((n * hd, length), f32), shape((n, length), f32), shape((n, length), f32)],
        )
        return first, token

    def far(c, token, first=()):
        n = sizes[c]
        args = (*kv(c), *first)
        pay, token = run(
            partial(far_kernel, scale2, n, not first, *even_place(c)),
            "far_pieces",
            1.5 * n,
            [loose, whole(entry), cols(c), kept, whole(ahead)] + [whole(a) for a in args],
            (token, entry, q_far, q_far, ahead, *args),
            [shape((n * hd + 16, length + hd), bf16)],
        )
        return shifted(pay, 2), token

    def merge(c, token):
        n = sizes[c]
        args = (pays[c], *parts[c])
        return run(
            partial(merge_kernel, n),
            "merge",
            0.5 * n,
            [loose, cols(c)] + [whole(a) for a in args],
            (token, query, *args),
            [shape((n * hd, length), f32), shape((1, length), f32)],
        )

    def gate(x, *after):
        return pl.pallas_call(
            gate_kernel,
            in_specs=[loose] * (1 + len(after)),
            out_specs=loose,
            out_shape=shape(x.shape, x.dtype),
            input_output_aliases={0: 0},
            compiler_params=params(1),
            name="gate",
        )(x, *after)

    chunks = range(len(sizes))
    diag, parts, pays = [None] * 3, [None] * 3, [None] * 3
    two_back, from_even, from_odd = [None] * 3, [None] * 2, [None] * 3
    two_back[0] = shifted(pay0, 2)
    from_even[0] = even_to_odd(pay0)
    diag[0], token = own(0, token)
    one, both, q_pay, token = run(
        partial(pack_kernel, sizes, width1),
        "pack",
        3,
        [loose, hbm, whole(keep), hbm, hbm, whole(dec)],
        (token, query, keep, key, value, dec),
        [pay_shape(1), shape((length + 32, width1 + pay_shape(2).shape[1]), bf16), shape((length + 16, features), bf16)],
        [dma((7,))],
    )
    two_back[1] = shifted(one, 2)
    from_odd[0] = odd_to_even(two_back[0])
    q_far = shifted(q_pay, -2)
    diag[1], token = own(1, token, two_back[0])
    dec_rows = pl.BlockSpec((16, length), lambda *_: (2, 0))
    pay, token = run(
        partial(pack_last_kernel, sizes), "pack", 1, [loose, hbm, hbm, dec_rows], (token, key, value, dec), [pay_shape(2)], [dma((2,))]
    )
    two_back[2] = shifted(pay, 2)
    from_even[1] = even_to_odd(both)
    from_odd[1] = odd_to_even(two_back[1])
    diag[2], token = own(2, token)
    pays[0], token = far(0, token)
    parts[0], token = near(0, token)
    two_back[2] = gate(two_back[2], token)
    from_odd[2] = odd_to_even(two_back[2])
    first, token = far_earlier(1, token)
    token = earlier(1, token)
    pays[1], token = far(1, token, first)
    parts[1], token = near(1, token)
    pays[2], token = far(2, token)
    parts[2], token = near(2, token)
    mixed, total = [], None
    for c in chunks:
        m, s, token = merge(c, token)
        mixed.append(m)
        total = s if total is None else total + s
    ranks = lax.axis_size("head")
    everyone = lax.all_gather(total.reshape(length // 128, 128), "head").reshape(ranks, length)
    gain = gain[None, :]
    return pl.pallas_call(
        partial(norm_kernel, len(mixed)),
        grid=(1,),
        in_specs=[whole(m) for m in mixed] + [whole(everyone), whole(gain)],
        out_specs=whole(query),
        out_shape=shape((length, features), bf16),
        compiler_params=params(),
        name="normalize",
    )(*mixed, everyone, gain)


def solution(mesh):
    placed = (
        P("ctx", "head"),
        P("ctx", "head"),
        P("ctx", "head"),
        P("head", "ctx"),
        P(),
        P("ctx", None),
        P("head"),
    )
    return jax.shard_map(on_device, mesh=mesh, in_specs=placed, out_specs=P("ctx", "head"), check_vma=False)
```

```python
import math
from functools import partial

import jax
import jax.numpy as jnp
from jax import lax
from jax.experimental import pallas as pl
from jax.experimental.pallas import tpu as pltpu
from jax.sharding import PartitionSpec as P

D = 4096
BLK = 128
REACH = 4
EPSILON = 1e-06
NEG = -1e30
FAR_OFF = 1 << 30
LOG2E = math.log2(math.e)

NT = (((1,), (1,)), ((), ()))
TN = (((0,), (0,)), ((), ()))
NN = (((1,), (0,)), ((), ()))


def dot(a, b, dims):
    return lax.dot_general(a, b, dims, preferred_element_type=jnp.float32)


def params(mib=24):
    return pltpu.CompilerParams(vmem_limit_bytes=mib * 1024 * 1024)


def shifted(x, by):
    n = lax.axis_size("ctx")
    return lax.ppermute(x, "ctx", [(i, i + by) for i in range(n) if 0 <= i + by < n])


def even_to_odd(x):
    n = lax.axis_size("ctx")
    return lax.ppermute(x, "ctx", [(i, i + 1) for i in range(0, n - 1, 2)])


def odd_to_even(x):
    n = lax.axis_size("ctx")
    return lax.ppermute(x, "ctx", [(i, i - 1) for i in range(1, n, 2)])


def split3(x):
    hi = x.astype(jnp.bfloat16)
    rest = x - hi.astype(jnp.float32)
    mid = rest.astype(jnp.bfloat16)
    low = (rest - mid.astype(jnp.float32)).astype(jnp.bfloat16)
    return hi.astype(jnp.float32), mid.astype(jnp.float32), low.astype(jnp.float32)


def split2(x):
    return split3(x)[:2]


def join2(rows, first):
    return rows[first : first + 1] + rows[first + 1 : first + 2]


def join3(rows, first):
    return rows[first : first + 1] + rows[first + 1 : first + 2] + rows[first + 2 : first + 3]


def stack_rows(rows, count, length):
    spot = lax.broadcasted_iota(jnp.int32, (count, length), 0)
    out = jnp.zeros((count, length), jnp.float32)
    for i, r in enumerate(rows):
        out = jnp.where(spot == i, r, out)
    return out


def softmax_of(parts, scale2):
    top = parts[0]
    for p in parts[1:]:
        top = jnp.maximum(top, p)
    top = jnp.max(top, axis=0, keepdims=True) * scale2
    weights = [jnp.exp2(p * scale2 - top) for p in parts]
    total = weights[0]
    for w in weights[1:]:
        total = total + w
    total = jnp.sum(total, axis=0, keepdims=True)
    return top, total, [w.astype(jnp.bfloat16) for w in weights]


def pick(rows, index):
    spot = lax.broadcasted_iota(jnp.int32, rows.shape, 0)
    return jnp.sum(jnp.where(spot == index, rows, 0.0), axis=0, keepdims=True)


def fetch(pay_ref, k_hbm, v_hbm, source, half, sems, first, at=0):
    length = k_hbm.shape[0]
    copies = []
    for i, hbm in enumerate((k_hbm, v_hbm)):
        lo = at + i * half
        target = pay_ref.at[0:length, lo : lo + half]
        copies.append(pltpu.make_async_copy(hbm.at[:, source : source + half], target, sems.at[first + i]))
        copies[-1].start()
    return copies


def fill(pay_ref, dec, length, dec_row):
    pay_ref[dec_row : dec_row + 16, 0:length] = dec
    if pay_ref.shape[1] > length:
        pay_ref[dec_row : dec_row + 16, length:] = jnp.zeros((16, pay_ref.shape[1] - length), jnp.bfloat16)


def running_sums(decays):
    heads, length = decays.shape
    parts = jnp.concatenate(split3(decays), axis=0).astype(jnp.bfloat16)
    u = lax.broadcasted_iota(jnp.int32, (length, length), 0)
    t = lax.broadcasted_iota(jnp.int32, (length, length), 1)
    ones = jnp.where(u <= t, 1.0, 0.0).astype(jnp.bfloat16)
    sums = dot(parts, ones, NN)
    return sums[:heads] + sums[heads : 2 * heads] + sums[2 * heads :]


def decay_rows(cum, first, n):
    length = cum.shape[1]
    last = cum[:, length - 1 :]
    rows = []
    for h in range(first, first + n):
        rows += list(split2(last[h : h + 1] - cum[h : h + 1]))
    for h in range(first, first + n):
        rows += list(split2(last[h : h + 1] + jnp.zeros((1, length), jnp.float32)))
    return stack_rows(rows, 16, length).astype(jnp.bfloat16)


def first_kernel(n, ld_hbm, k_hbm, v_hbm, pay_hbm, token_ref, ld_ref, stage_ref, sems):
    length = k_hbm.shape[0]
    half = n * 128
    decays = pltpu.make_async_copy(ld_hbm, ld_ref, sems.at[0])
    decays.start()
    loads = fetch(stage_ref, k_hbm, v_hbm, 0, half, sems, 1)
    decays.wait()
    fill(stage_ref, decay_rows(running_sums(ld_ref[...]), 0, n), length, length)
    stores = [pltpu.make_async_copy(stage_ref.at[length : length + 16, :], pay_hbm.at[length : length + 16, :], sems.at[3])]
    stores[-1].start()
    for i in range(2):
        loads[i].wait()
        where = (slice(0, length), slice(i * half, (i + 1) * half))
        stores.append(pltpu.make_async_copy(stage_ref.at[where], pay_hbm.at[where], sems.at[4 + i]))
        stores[-1].start()
    token_ref[...] = jnp.zeros_like(token_ref)
    for store in stores:
        store.wait()


def prep_kernel(
    divisor, sizes, token_in, docs_ref, mask_ref, ld_ref,
    thr_ref, start_ref, ahead_ref, entry_ref, keep_ref, cum_ref, cumt_ref, coef_ref, dec_ref, token_ref,
):
    heads, length = ld_ref.shape
    tiles = length // BLK
    begin = lax.axis_index("ctx").astype(jnp.int32) * length
    f32, bf16 = jnp.float32, jnp.bfloat16
    cum = running_sums(ld_ref[...])
    cum_ref[...] = cum
    cumt_ref[...] = jnp.concatenate([cum, jnp.zeros((BLK - heads, length), f32)], axis=0).T
    pos = begin + lax.broadcasted_iota(jnp.int32, (8, length), 1)
    start = jnp.zeros((8, length), jnp.int32)
    ahead = jnp.zeros((8, length), jnp.int32)
    entry = jnp.zeros((8, length), jnp.int32)
    end = jnp.zeros((1, 1), jnp.int32)
    for d in range(docs_ref.shape[1]):
        end = end + docs_ref[:, d : d + 1]
        start = jnp.where(pos >= end, end, start)
        ahead = jnp.where(pos + 2 * length >= end, end, ahead)
        entry = jnp.where(begin - 1 >= end, end, entry)
    start = start - begin
    start_ref[...] = start
    ahead_ref[...] = ahead - (begin + 2 * length)
    entry_ref[...] = entry - begin
    coef_ref[...] = jnp.exp(cum) * jnp.where(start[:1] < 0, 1.0 / divisor, 0.0)
    reach = mask_ref.shape[1]
    tile_row = lax.broadcasted_iota(jnp.int32, (reach, length), 0)
    tile_of = lax.broadcasted_iota(jnp.int32, (reach, length), 1) // BLK
    spread = (lax.broadcasted_iota(jnp.int32, (tiles, length), 1) // BLK == lax.broadcasted_iota(jnp.int32, (tiles, length), 0))
    picked = dot(mask_ref[...].astype(f32).astype(bf16), jnp.where(spread, 1.0, 0.0).astype(bf16), TN)
    keep = (picked > 0.5) | (tile_row == REACH * tiles + tile_of)
    base = (tile_row - REACH * tiles) * BLK
    thr_ref[...] = jnp.where(keep, start[:1] - base, FAR_OFF)
    kept = jnp.where(picked > 0.5, 1.0, 0.0)
    keep_ref[...] = kept[0:16].astype(bf16)
    first = 0
    for c, n in enumerate(sizes):
        dec_ref[c * 16 : (c + 1) * 16, :] = decay_rows(cum, first, n)
        first += n
    token_ref[...] = jnp.zeros_like(token_ref)


def pack_kernel(sizes, width1, token_in, q_ref, keep_ref, k_ref, v_ref, dec_ref, one_ref, both_ref, qpay_ref, token_ref, sems):
    length, features = q_ref.shape
    first, second = sizes[0] * 128, (sizes[0] + sizes[1]) * 128
    copies = fetch(one_ref, k_ref, v_ref, first, sizes[1] * 128, sems, 0)
    copies.append(pltpu.make_async_copy(q_ref, qpay_ref.at[0:length, :], sems.at[6]))
    copies[-1].start()
    copies += fetch(both_ref, k_ref, v_ref, first, sizes[1] * 128, sems, 2)
    copies += fetch(both_ref, k_ref, v_ref, second, sizes[2] * 128, sems, 4, width1)
    fill(one_ref, dec_ref[16:32, :], length, length)
    fill(both_ref, dec_ref[16:32, :], length, length)
    fill(both_ref, dec_ref[32:48, :], length, length + 16)
    qpay_ref[length:, 0:length] = keep_ref[...]
    if features > length:
        qpay_ref[length:, length:] = jnp.zeros((16, features - length), jnp.bfloat16)
    token_ref[...] = jnp.zeros_like(token_ref)
    for copy in copies:
        copy.wait()


def pack_last_kernel(sizes, token_in, k_ref, v_ref, dec_ref, pay_ref, token_ref, sems):
    length = k_ref.shape[0]
    copies = fetch(pay_ref, k_ref, v_ref, (sizes[0] + sizes[1]) * 128, sizes[2] * 128, sems, 0)
    fill(pay_ref, dec_ref[...], length, length)
    token_ref[...] = jnp.zeros_like(token_ref)
    for copy in copies:
        copy.wait()


def gate_kernel(*refs):
    pass


def own_kernel(scale2, divisor, n, base, q_hbm, k_hbm, v_hbm, thr_ref, start_ref, cum_ref, cumt_ref, o_ref, top_ref, tot_ref, lin_ref, token_ref, held, sems):
    length = q_hbm.shape[0]
    tiles = length // BLK
    own = REACH * tiles
    copies = []
    for i in range(n):
        h = base + i
        for part, hbm in enumerate((q_hbm, k_hbm, v_hbm)):
            source = hbm.at[:, h * 128 : (h + 1) * 128]
            copies.append(pltpu.make_async_copy(source, held.at[3 * i + part], sems.at[3 * i + part]))
            copies[-1].start()
    row = lax.broadcasted_iota(jnp.int32, (BLK, length), 0)
    col = lax.broadcasted_iota(jnp.int32, (BLK, length), 1)
    for i in range(n):
        h = base + i
        for copy in copies[3 * i : 3 * i + 3]:
            copy.wait()
        q, k, v = held[3 * i], held[3 * i + 1], held[3 * i + 2]
        scores = dot(k, q, NT)
        cum_row = cum_ref[h : h + 1, :]
        soft, mix = [], []
        for j in range(tiles):
            s = scores[j * BLK : (j + 1) * BLK]
            causal = row <= col - j * BLK
            soft.append(jnp.where(causal & (row >= thr_ref[own + j : own + j + 1, :]), s, NEG))
            gap = cum_row - cumt_ref[j * BLK : (j + 1) * BLK, h : h + 1]
            ok = causal & (row >= start_ref[0:1, :] - j * BLK)
            decay = jnp.exp(jnp.where(ok, gap, NEG))
            mix.append((s * decay * (1.0 / divisor)).astype(jnp.bfloat16))
        top, total, weights = softmax_of(soft, scale2)
        rows = slice(i * 128, (i + 1) * 128)
        o_ref[rows, :] = dot(v, jnp.concatenate(weights, axis=0), TN)
        lin_ref[rows, :] = dot(v, jnp.concatenate(mix, axis=0), TN)
        top_ref[i : i + 1, :] = top
        tot_ref[i : i + 1, :] = total
    token_ref[...] = jnp.zeros_like(token_ref)


def partial_softmax(q, groups, thr, scale2):
    tiles = groups[0][1].shape[0] // BLK
    row = lax.broadcasted_iota(jnp.int32, (BLK, q.shape[0]), 0)
    parts = []
    for first, keys, _ in groups:
        scores = dot(keys, q, NT)
        for j in range(tiles):
            ok = row >= thr[first + j : first + j + 1]
            parts.append(jnp.where(ok, scores[j * BLK : (j + 1) * BLK], NEG))
    top, total, weights = softmax_of(parts, scale2)
    o = None
    for g, (_, _, values) in enumerate(groups):
        here = dot(values, jnp.concatenate(weights[g * tiles : (g + 1) * tiles], axis=0), TN)
        o = here if o is None else o + here
    return top, total, o


def earlier_kernel(scale2, n, token_in, q_ref, thr_ref, two, od_ref, topd_ref, totd_ref, o_ref, top_ref, tot_ref, token_ref):
    length = q_ref.shape[0]
    thr = thr_ref[...]
    for i in range(n):
        rows = slice(i * 128, (i + 1) * 128)
        keys = two[0:length, i * 128 : (i + 1) * 128]
        values = two[0:length, (n + i) * 128 : (n + i + 1) * 128]
        top, total, o = partial_softmax(q_ref[:, rows], [(0, keys, values)], thr, scale2)
        top_d = topd_ref[i : i + 1, :]
        new_top = jnp.maximum(top, top_d)
        a, b = jnp.exp2(top - new_top), jnp.exp2(top_d - new_top)
        o_ref[rows, :] = o * a + od_ref[rows, :] * b
        top_ref[i : i + 1, :] = new_top
        tot_ref[i : i + 1, :] = total * a + totd_ref[i : i + 1, :] * b
    token_ref[...] = jnp.zeros_like(token_ref)


class Pieces:
    def __init__(self, n, two, even, odd, entry, even_at, even_dec):
        self.n, self.two, self.even, self.odd, self.even_at = n, two, even, odd, even_at
        length = self.length = odd.shape[0] - 16
        rows2 = two[length:, 0:length].astype(jnp.float32)
        rows1 = (even[even_dec : even_dec + 16, 0:length] + odd[length:, 0:length]).astype(jnp.float32)
        self.tot1 = [join2(rows1, 2 * n + 2 * i) for i in range(n)]
        self.tot2 = [join2(rows2, 2 * n + 2 * i) for i in range(n)]
        after1 = [join2(rows1, 2 * i) for i in range(n)]
        after2 = [join2(rows2, 2 * i) + self.tot1[i] for i in range(n)]
        col = lax.broadcasted_iota(jnp.int32, (1, length), 1)
        w1 = [jnp.where(col - length >= entry, jnp.exp(x), 0.0) for x in after1]
        w2 = [jnp.where(col - 2 * length >= entry, jnp.exp(x), 0.0) for x in after2]
        self.weight = stack_rows(w1 + w2, BLK, length).T

    def part(self, index):
        cols = slice(index * 128, (index + 1) * 128)
        at = slice(self.even_at + index * 128, self.even_at + (index + 1) * 128)
        return self.two[0 : self.length, cols], self.even[0 : self.length, at] + self.odd[0 : self.length, cols]

    def attend(self, i, q, thr, scale2, both=True):
        tiles = self.length // BLK
        k2, k1 = self.part(i)
        v2, v1 = self.part(self.n + i)
        groups = [(0, k2, v2), (tiles, k1, v1)] if both else [(tiles, k1, v1)]
        top, total, o = partial_softmax(q, groups, thr, scale2)
        n = self.n
        kw1 = (k1.astype(jnp.float32) * self.weight[:, i : i + 1]).astype(jnp.bfloat16)
        kw2 = (k2.astype(jnp.float32) * self.weight[:, n + i : n + i + 1]).astype(jnp.bfloat16)
        state = dot(v2, kw2, TN) + dot(v1, kw1, TN)
        return top, total, o, state.astype(jnp.bfloat16)


def far_thresholds(keep_ref, ahead_ref):
    keep = keep_ref[...].astype(jnp.float32)
    tiles = keep.shape[1] // BLK
    thr = []
    for j in range(2 * tiles):
        base = (j - REACH * tiles) * BLK
        thr.append(jnp.where(keep[j : j + 1] > 0.5, ahead_ref[0:1, :] - base, FAR_OFF))
    return jnp.concatenate(thr, axis=0)


def far_earlier_kernel(scale2, n, token_in, q_ref, keep_ref, ahead_ref, two, o_ref, top_ref, tot_ref, token_ref):
    thr = far_thresholds(keep_ref, ahead_ref)
    length = thr.shape[1]
    for i in range(n):
        rows = slice(i * 128, (i + 1) * 128)
        keys = two[0:length, i * 128 : (i + 1) * 128]
        values = two[0:length, (n + i) * 128 : (n + i + 1) * 128]
        top, total, o = partial_softmax(q_ref[0:length, rows], [(0, keys, values)], thr, scale2)
        o_ref[rows, :] = o
        top_ref[i : i + 1, :] = top
        tot_ref[i : i + 1, :] = total
    token_ref[...] = jnp.zeros_like(token_ref)


def far_kernel(scale2, n, both, even_at, even_dec, token_in, entry_ref, q_ref, keep_ref, ahead_ref, two, even, odd, *rest):
    out_ref, token_ref = rest[-2:]
    p = Pieces(n, two, even, odd, entry_ref[0:1, :], even_at, even_dec)
    length = p.length
    thr = far_thresholds(keep_ref, ahead_ref)
    rows = [jnp.ones((1, length), jnp.float32)]
    for i in range(n):
        top, total, o, state = p.attend(i, q_ref[0:length, i * 128 : (i + 1) * 128], thr, scale2, both)
        if not both:
            o_e, top_e, tot_e = rest[0][i * 128 : (i + 1) * 128, :], rest[1][i : i + 1, :], rest[2][i : i + 1, :]
            new_top = jnp.maximum(top, top_e)
            a, b = jnp.exp2(top - new_top), jnp.exp2(top_e - new_top)
            top, total, o = new_top, total * a + tot_e * b, o * a + o_e * b
        r = i * 128
        out_ref[r : r + 128, 0:length] = (o * (1.0 / total)).astype(jnp.bfloat16)
        out_ref[r : r + 128, length:] = state
        lse = top + jnp.log(total) * LOG2E
        rows += list(split3(lse))
    out_ref[n * 128 :, 0:length] = stack_rows(rows, 16, length).astype(jnp.bfloat16)
    out_ref[n * 128 :, length:] = jnp.zeros((16, 128), jnp.bfloat16)
    token_ref[...] = jnp.zeros_like(token_ref)


def near_kernel(
    scale2, n, first, both, even_at, even_dec, token_in, entry_ref, q_ref, thr_ref, coef_ref, two, even, odd, od_ref, topd_ref, totd_ref, lind_ref,
    x_ref, on_ref, st_ref, token_ref,
):
    entry = entry_ref[0:1, :]
    p = Pieces(n, two, even, odd, entry, even_at, even_dec)
    length = p.length
    lses, coefs = [], []
    thr = thr_ref[...]
    for i in range(n):
        q = q_ref[:, i * 128 : (i + 1) * 128]
        rows = slice(i * 128, (i + 1) * 128)
        top, total, o, state = p.attend(i, q, thr, scale2, both)
        top_d = topd_ref[i : i + 1, :]
        new_top = jnp.maximum(top, top_d)
        a, b = jnp.exp2(top - new_top), jnp.exp2(top_d - new_top)
        total = total * a + totd_ref[i : i + 1, :] * b
        inv = 1.0 / total
        on = o * (a * inv) + od_ref[rows, :] * (b * inv)
        coef = coef_ref[first + i : first + i + 1, :]
        x_ref[rows, :] = lind_ref[rows, :] + dot(state, q, NT) * coef + on
        on_ref[rows, :] = on
        lses.append(new_top + jnp.log(total) * LOG2E)
        through = jnp.where(entry < -2 * length, jnp.exp(p.tot1[i] + p.tot2[i]), 0.0)
        coefs.append(coef * through)
    st_ref[...] = stack_rows(lses + coefs, 8, length)
    token_ref[...] = jnp.zeros_like(token_ref)


def merge_kernel(n, token_in, q_ref, pay_ref, x_ref, on_ref, st_ref, mixed_ref, sq_ref, token_ref):
    squares = None
    length = q_ref.shape[0]
    stats = pay_ref[n * 128 :, 0:length].astype(jnp.float32)
    for i in range(n):
        q = q_ref[:, i * 128 : (i + 1) * 128]
        rows = slice(i * 128, (i + 1) * 128)
        lse_far = join3(stats, 1 + 3 * i)
        far = pay_ref[rows, 0:length].astype(jnp.float32)
        share = 1.0 / (1.0 + jnp.exp2(jnp.minimum(st_ref[i : i + 1, :] - lse_far, 120.0)))
        share = jnp.where((lse_far > 0.5 * NEG) & (stats[0:1] > 0.5), share, 0.0)
        lin = dot(pay_ref[rows, length:], q, NT) * st_ref[n + i : n + i + 1, :]
        mixed = x_ref[rows, :] + share * (far - on_ref[rows, :]) + lin
        mixed_ref[:, rows] = mixed.T
        part = jnp.sum(mixed * mixed, axis=0, keepdims=True)
        squares = part if squares is None else squares + part
    sq_ref[...] = squares
    token_ref[...] = jnp.zeros_like(token_ref)


def norm_kernel(parts, *refs):
    mixed_refs, sq_ref, gain_ref, out_ref = refs[:parts], refs[parts], refs[parts + 1], refs[parts + 2]
    inverse = lax.rsqrt(jnp.sum(sq_ref[...], axis=0, keepdims=True) / D + EPSILON)
    spread = (jnp.zeros((128, inverse.shape[1]), jnp.float32) + inverse).T
    col = 0
    for ref in mixed_refs:
        for i in range(ref.shape[1] // 128):
            part = ref[:, i * 128 : (i + 1) * 128] * spread
            out_ref[:, col : col + 128] = (part * gain_ref[:, col : col + 128]).astype(jnp.bfloat16)
            col += 128


def on_device(query, key, value, log_decay, doc_lengths, tile_mask, gain):
    length, features = query.shape
    heads = log_decay.shape[0]
    hd = features // heads
    tiles = length // BLK
    sizes = [(heads + 2) // 3, (heads + 1) // 3, heads // 3]
    firsts = [sum(sizes[:c]) for c in range(len(sizes))]
    divisor = hd * math.sqrt(length)
    scale2 = LOG2E / math.sqrt(hd)
    f32, bf16 = jnp.float32, jnp.bfloat16
    shape = jax.ShapeDtypeStruct
    loose = pl.BlockSpec(memory_space=pl.ANY)
    hbm = pl.BlockSpec(memory_space=pltpu.HBM)
    dma = pltpu.SemaphoreType.DMA

    def whole(x):
        return pl.BlockSpec(x.shape, lambda *_: (0,) * len(x.shape))

    def cols(c, rows=length):
        return pl.BlockSpec((rows, sizes[c] * hd), lambda *_: (0, firsts[c] // sizes[c]))

    def run(kernel, name, us, specs, args, outs, scratch=(), limit=24, out_specs=None):
        outs = outs + [shape((8, 128), f32)]
        out_specs = (out_specs or [whole(o) for o in outs[:-1]]) + [whole(outs[-1])]
        return pl.pallas_call(
            kernel,
            grid=(1,),
            in_specs=specs,
            out_specs=out_specs,
            out_shape=outs,
            scratch_shapes=scratch,
            compiler_params=params(limit),
            cost_estimate=pl.CostEstimate(flops=0, bytes_accessed=int(us * 3.69e6), transcendentals=0),
            name=name,
        )(*args)

    def pay_shape(c):
        return shape((length + 16, max(length, 2 * sizes[c] * hd)), bf16)

    docs = doc_lengths[None, :]
    outs = [
        shape(((REACH + 1) * tiles, length), jnp.int32),
        shape((8, length), jnp.int32),
        shape((8, length), jnp.int32),
        shape((8, length), jnp.int32),
        shape((16, length), bf16),
        shape((heads, length), f32),
        shape((length, BLK), f32),
        shape((heads, length), f32),
        shape((16 * len(sizes), length), bf16),
    ]
    pay0, token = run(
        partial(first_kernel, sizes[0]),
        "first_chunk",
        1,
        [hbm, hbm, hbm],
        (log_decay, key, value),
        [pay_shape(0)],
        [pltpu.VMEM(log_decay.shape, f32), pltpu.VMEM(pay_shape(0).shape, bf16), dma((6,))],
        limit=60,
        out_specs=[hbm],
    )
    thr, start, ahead, entry, keep, cum, cum_t, coef, dec, token = run(
        partial(prep_kernel, divisor, sizes),
        "prep",
        2,
        [loose, whole(docs), whole(tile_mask), whole(log_decay)],
        (token, docs, tile_mask, log_decay),
        outs,
    )
    thr_near = pl.BlockSpec((2 * tiles, length), lambda *_: (1, 0))

    def own(c, token, *after):
        n, first = sizes[c], firsts[c]
        outs = [shape((n * hd, length), f32), shape((n, length), f32), shape((n, length), f32), shape((n * hd, length), f32)]

        def kernel(*refs):
            own_kernel(scale2, divisor, n, first, *refs[len(after) + 1 :])

        *result, token = run(
            kernel,
            "own_piece",
            n * 0.8,
            [loose] * (len(after) + 1) + [hbm] * 3 + [whole(thr), whole(start), whole(cum), whole(cum_t)],
            (*after, token, query, key, value, thr, start, cum, cum_t),
            outs,
            [pltpu.VMEM((3 * n, length, hd), bf16), dma((3 * n,))],
        )
        return result, token

    width1 = pay_shape(1).shape[1]

    def kv(c):
        return two_back[c], from_even[min(c, 1)], from_odd[c]

    def even_place(c):
        return (0, length) if c < 2 else (width1, length + 16)

    def near(c, token):
        n = sizes[c]
        args = (*kv(c), *diag[c])
        x, on, st, token = run(
            partial(near_kernel, scale2, n, firsts[c], c != 1, *even_place(c)),
            "near_pieces",
            1.8 * n,
            [loose, whole(entry), cols(c), thr_near, whole(coef)] + [whole(a) for a in args],
            (token, entry, query, thr, coef, *args),
            [shape((n * hd, length), f32), shape((n * hd, length), f32), shape((8, length), f32)],
        )
        return (x, on, st), token

    def earlier(c, token):
        n = sizes[c]
        args = (two_back[c], *diag[c][:3])
        o, top, tot, token = run(
            partial(earlier_kernel, scale2, n),
            "earlier_piece",
            0.8 * n,
            [loose, cols(c), thr_near] + [whole(a) for a in args],
            (token, query, thr, *args),
            [shape((n * hd, length), f32), shape((n, length), f32), shape((n, length), f32)],
        )
        diag[c] = [o, top, tot, diag[c][3]]
        return token

    kept = pl.BlockSpec((16, length), lambda *_: (length // 16, 0))

    def far_earlier(c, token):
        n = sizes[c]
        *first, token = run(
            partial(far_earlier_kernel, scale2, n),
            "far_earlier",
            0.7 * n,
            [loose, cols(c), kept, whole(ahead), whole(two_back[c])],
            (token, q_far, q_far, ahead, two_back[c]),
            [shape((n * hd, length), f32), shape((n, length), f32), shape((n, length), f32)],
        )
        return first, token

    def far(c, token, first=()):
        n = sizes[c]
        args = (*kv(c), *first)
        pay, token = run(
            partial(far_kernel, scale2, n, not first, *even_place(c)),
            "far_pieces",
            1.5 * n,
            [loose, whole(entry), cols(c), kept, whole(ahead)] + [whole(a) for a in args],
            (token, entry, q_far, q_far, ahead, *args),
            [shape((n * hd + 16, length + hd), bf16)],
        )
        return shifted(pay, 2), token

    def merge(c, token):
        n = sizes[c]
        args = (pays[c], *parts[c])
        return run(
            partial(merge_kernel, n),
            "merge",
            0.5 * n,
            [loose, cols(c)] + [whole(a) for a in args],
            (token, query, *args),
            [shape((length, n * hd), f32), shape((1, length), f32)],
        )

    def gate(x, *after):
        return pl.pallas_call(
            gate_kernel,
            in_specs=[loose] * (1 + len(after)),
            out_specs=loose,
            out_shape=shape(x.shape, x.dtype),
            input_output_aliases={0: 0},
            compiler_params=params(1),
            name="gate",
        )(x, *after)

    chunks = range(len(sizes))
    diag, parts, pays = [None] * 3, [None] * 3, [None] * 3
    two_back, from_even, from_odd = [None] * 3, [None] * 2, [None] * 3
    two_back[0] = shifted(pay0, 2)
    from_even[0] = even_to_odd(pay0)
    diag[0], token = own(0, token)
    one, both, q_pay, token = run(
        partial(pack_kernel, sizes, width1),
        "pack",
        3,
        [loose, hbm, whole(keep), hbm, hbm, whole(dec)],
        (token, query, keep, key, value, dec),
        [pay_shape(1), shape((length + 32, width1 + pay_shape(2).shape[1]), bf16), shape((length + 16, features), bf16)],
        [dma((7,))],
    )
    two_back[1] = shifted(one, 2)
    from_odd[0] = odd_to_even(two_back[0])
    q_far = shifted(q_pay, -2)
    diag[1], token = own(1, token, two_back[0])
    dec_rows = pl.BlockSpec((16, length), lambda *_: (2, 0))
    pay, token = run(
        partial(pack_last_kernel, sizes), "pack", 1, [loose, hbm, hbm, dec_rows], (token, key, value, dec), [pay_shape(2)], [dma((2,))]
    )
    two_back[2] = shifted(pay, 2)
    from_even[1] = even_to_odd(both)
    from_odd[1] = odd_to_even(two_back[1])
    diag[2], token = own(2, token)
    pays[0], token = far(0, token)
    parts[0], token = near(0, token)
    two_back[2] = gate(two_back[2], token)
    from_odd[2] = odd_to_even(two_back[2])
    first, token = far_earlier(1, token)
    token = earlier(1, token)
    pays[1], token = far(1, token, first)
    parts[1], token = near(1, token)
    pays[2], token = far(2, token)
    parts[2], token = near(2, token)
    mixed, total = [], None
    for c in chunks:
        m, s, token = merge(c, token)
        mixed.append(m)
        total = s if total is None else total + s
    ranks = lax.axis_size("head")
    everyone = lax.all_gather(total.reshape(length // 128, 128), "head").reshape(ranks, length)
    gain = gain[None, :]
    return pl.pallas_call(
        partial(norm_kernel, len(mixed)),
        grid=(1,),
        in_specs=[whole(m) for m in mixed] + [whole(everyone), whole(gain)],
        out_specs=whole(query),
        out_shape=shape((length, features), bf16),
        compiler_params=params(),
        name="normalize",
    )(*mixed, everyone, gain)


def solution(mesh):
    placed = (
        P("ctx", "head"),
        P("ctx", "head"),
        P("ctx", "head"),
        P("head", "ctx"),
        P(),
        P("ctx", None),
        P("head"),
    )
    return jax.shard_map(on_device, mesh=mesh, in_specs=placed, out_specs=P("ctx", "head"), check_vma=False)
```

```python
import math
from functools import partial

import jax
import jax.numpy as jnp
from jax import lax
from jax.experimental import pallas as pl
from jax.experimental.pallas import tpu as pltpu
from jax.sharding import PartitionSpec as P

D = 4096
BLK = 128
REACH = 4
EPSILON = 1e-06
NEG = -1e30
FAR_OFF = 1 << 30
LOG2E = math.log2(math.e)

NT = (((1,), (1,)), ((), ()))
TN = (((0,), (0,)), ((), ()))
NN = (((1,), (0,)), ((), ()))


def dot(a, b, dims):
    return lax.dot_general(a, b, dims, preferred_element_type=jnp.float32)


def params(mib=24):
    return pltpu.CompilerParams(vmem_limit_bytes=mib * 1024 * 1024)


def shifted(x, by):
    n = lax.axis_size("ctx")
    return lax.ppermute(x, "ctx", [(i, i + by) for i in range(n) if 0 <= i + by < n])


def even_to_odd(x):
    n = lax.axis_size("ctx")
    return lax.ppermute(x, "ctx", [(i, i + 1) for i in range(0, n - 1, 2)])


def odd_to_even(x):
    n = lax.axis_size("ctx")
    return lax.ppermute(x, "ctx", [(i, i - 1) for i in range(1, n, 2)])


def split3(x):
    hi = x.astype(jnp.bfloat16)
    rest = x - hi.astype(jnp.float32)
    mid = rest.astype(jnp.bfloat16)
    low = (rest - mid.astype(jnp.float32)).astype(jnp.bfloat16)
    return hi.astype(jnp.float32), mid.astype(jnp.float32), low.astype(jnp.float32)


def split2(x):
    return split3(x)[:2]


def join2(rows, first):
    return rows[first : first + 1] + rows[first + 1 : first + 2]


def join3(rows, first):
    return rows[first : first + 1] + rows[first + 1 : first + 2] + rows[first + 2 : first + 3]


def stack_rows(rows, count, length):
    spot = lax.broadcasted_iota(jnp.int32, (count, length), 0)
    out = jnp.zeros((count, length), jnp.float32)
    for i, r in enumerate(rows):
        out = jnp.where(spot == i, r, out)
    return out


def softmax_of(parts, scale2):
    top = parts[0]
    for p in parts[1:]:
        top = jnp.maximum(top, p)
    top = jnp.max(top, axis=0, keepdims=True) * scale2
    weights = [jnp.exp2(p * scale2 - top) for p in parts]
    total = weights[0]
    for w in weights[1:]:
        total = total + w
    total = jnp.sum(total, axis=0, keepdims=True)
    return top, total, [w.astype(jnp.bfloat16) for w in weights]


def pick(rows, index):
    spot = lax.broadcasted_iota(jnp.int32, rows.shape, 0)
    return jnp.sum(jnp.where(spot == index, rows, 0.0), axis=0, keepdims=True)


def fetch(pay_ref, k_hbm, v_hbm, source, half, sems, first, at=0):
    length = k_hbm.shape[0]
    copies = []
    for i, hbm in enumerate((k_hbm, v_hbm)):
        lo = at + i * half
        target = pay_ref.at[0:length, lo : lo + half]
        copies.append(pltpu.make_async_copy(hbm.at[:, source : source + half], target, sems.at[first + i]))
        copies[-1].start()
    return copies


def fill(pay_ref, dec, length, dec_row):
    pay_ref[dec_row : dec_row + 16, 0:length] = dec
    if pay_ref.shape[1] > length:
        pay_ref[dec_row : dec_row + 16, length:] = jnp.zeros((16, pay_ref.shape[1] - length), jnp.bfloat16)


def running_sums(decays):
    heads, length = decays.shape
    parts = jnp.concatenate(split3(decays), axis=0).astype(jnp.bfloat16)
    u = lax.broadcasted_iota(jnp.int32, (length, length), 0)
    t = lax.broadcasted_iota(jnp.int32, (length, length), 1)
    ones = jnp.where(u <= t, 1.0, 0.0).astype(jnp.bfloat16)
    sums = dot(parts, ones, NN)
    return sums[:heads] + sums[heads : 2 * heads] + sums[2 * heads :]


def decay_rows(cum, first, n):
    length = cum.shape[1]
    last = cum[:, length - 1 :]
    rows = []
    for h in range(first, first + n):
        rows += list(split2(last[h : h + 1] - cum[h : h + 1]))
    for h in range(first, first + n):
        rows += list(split2(last[h : h + 1] + jnp.zeros((1, length), jnp.float32)))
    return stack_rows(rows, 16, length).astype(jnp.bfloat16)


def first_kernel(n, ld_hbm, k_hbm, v_hbm, pay_hbm, token_ref, ld_ref, stage_ref, sems):
    length = k_hbm.shape[0]
    half = n * 128
    decays = pltpu.make_async_copy(ld_hbm, ld_ref, sems.at[0])
    decays.start()
    loads = fetch(stage_ref, k_hbm, v_hbm, 0, half, sems, 1)
    decays.wait()
    fill(stage_ref, decay_rows(running_sums(ld_ref[...]), 0, n), length, length)
    stores = [pltpu.make_async_copy(stage_ref.at[length : length + 16, :], pay_hbm.at[length : length + 16, :], sems.at[3])]
    stores[-1].start()
    for i in range(2):
        loads[i].wait()
        where = (slice(0, length), slice(i * half, (i + 1) * half))
        stores.append(pltpu.make_async_copy(stage_ref.at[where], pay_hbm.at[where], sems.at[4 + i]))
        stores[-1].start()
    token_ref[...] = jnp.zeros_like(token_ref)
    for store in stores:
        store.wait()


def prep_kernel(
    divisor, sizes, token_in, docs_ref, mask_ref, ld_ref,
    thr_ref, start_ref, ahead_ref, entry_ref, keep_ref, cum_ref, cumt_ref, coef_ref, dec_ref, token_ref,
):
    heads, length = ld_ref.shape
    tiles = length // BLK
    begin = lax.axis_index("ctx").astype(jnp.int32) * length
    f32, bf16 = jnp.float32, jnp.bfloat16
    cum = running_sums(ld_ref[...])
    cum_ref[...] = cum
    cumt_ref[...] = jnp.concatenate([cum, jnp.zeros((BLK - heads, length), f32)], axis=0).T
    pos = begin + lax.broadcasted_iota(jnp.int32, (8, length), 1)
    start = jnp.zeros((8, length), jnp.int32)
    ahead = jnp.zeros((8, length), jnp.int32)
    entry = jnp.zeros((8, length), jnp.int32)
    end = jnp.zeros((1, 1), jnp.int32)
    for d in range(docs_ref.shape[1]):
        end = end + docs_ref[:, d : d + 1]
        start = jnp.where(pos >= end, end, start)
        ahead = jnp.where(pos + 2 * length >= end, end, ahead)
        entry = jnp.where(begin - 1 >= end, end, entry)
    start = start - begin
    start_ref[...] = start
    ahead_ref[...] = ahead - (begin + 2 * length)
    entry_ref[...] = entry - begin
    coef_ref[...] = jnp.exp(cum) * jnp.where(start[:1] < 0, 1.0 / divisor, 0.0)
    reach = mask_ref.shape[1]
    tile_row = lax.broadcasted_iota(jnp.int32, (reach, length), 0)
    tile_of = lax.broadcasted_iota(jnp.int32, (reach, length), 1) // BLK
    spread = (lax.broadcasted_iota(jnp.int32, (tiles, length), 1) // BLK == lax.broadcasted_iota(jnp.int32, (tiles, length), 0))
    picked = dot(mask_ref[...].astype(f32).astype(bf16), jnp.where(spread, 1.0, 0.0).astype(bf16), TN)
    keep = (picked > 0.5) | (tile_row == REACH * tiles + tile_of)
    base = (tile_row - REACH * tiles) * BLK
    thr_ref[...] = jnp.where(keep, start[:1] - base, FAR_OFF)
    kept = jnp.where(picked > 0.5, 1.0, 0.0)
    keep_ref[...] = kept[0:16].astype(bf16)
    first = 0
    for c, n in enumerate(sizes):
        dec_ref[c * 16 : (c + 1) * 16, :] = decay_rows(cum, first, n)
        first += n
    token_ref[...] = jnp.zeros_like(token_ref)


def pack_kernel(sizes, width1, token_in, q_ref, keep_ref, k_ref, v_ref, dec_ref, one_ref, both_ref, qpay_ref, token_ref, sems):
    length, features = q_ref.shape
    first, second = sizes[0] * 128, (sizes[0] + sizes[1]) * 128
    copies = fetch(one_ref, k_ref, v_ref, first, sizes[1] * 128, sems, 0)
    copies.append(pltpu.make_async_copy(q_ref, qpay_ref.at[0:length, :], sems.at[6]))
    copies[-1].start()
    copies += fetch(both_ref, k_ref, v_ref, first, sizes[1] * 128, sems, 2)
    copies += fetch(both_ref, k_ref, v_ref, second, sizes[2] * 128, sems, 4, width1)
    fill(one_ref, dec_ref[16:32, :], length, length)
    fill(both_ref, dec_ref[16:32, :], length, length)
    fill(both_ref, dec_ref[32:48, :], length, length + 16)
    qpay_ref[length:, 0:length] = keep_ref[...]
    if features > length:
        qpay_ref[length:, length:] = jnp.zeros((16, features - length), jnp.bfloat16)
    token_ref[...] = jnp.zeros_like(token_ref)
    for copy in copies:
        copy.wait()


def pack_last_kernel(sizes, token_in, k_ref, v_ref, dec_ref, pay_ref, token_ref, sems):
    length = k_ref.shape[0]
    copies = fetch(pay_ref, k_ref, v_ref, (sizes[0] + sizes[1]) * 128, sizes[2] * 128, sems, 0)
    fill(pay_ref, dec_ref[...], length, length)
    token_ref[...] = jnp.zeros_like(token_ref)
    for copy in copies:
        copy.wait()


def gate_kernel(*refs):
    pass


def own_kernel(scale2, divisor, n, base, q_hbm, k_hbm, v_hbm, thr_ref, start_ref, cum_ref, cumt_ref, o_ref, top_ref, tot_ref, lin_ref, token_ref, held, sems):
    length = q_hbm.shape[0]
    tiles = length // BLK
    own = REACH * tiles
    copies = []
    for i in range(n):
        h = base + i
        for part, hbm in enumerate((q_hbm, k_hbm, v_hbm)):
            source = hbm.at[:, h * 128 : (h + 1) * 128]
            copies.append(pltpu.make_async_copy(source, held.at[3 * i + part], sems.at[3 * i + part]))
            copies[-1].start()
    row = lax.broadcasted_iota(jnp.int32, (BLK, length), 0)
    col = lax.broadcasted_iota(jnp.int32, (BLK, length), 1)
    for i in range(n):
        h = base + i
        for copy in copies[3 * i : 3 * i + 3]:
            copy.wait()
        q, k, v = held[3 * i], held[3 * i + 1], held[3 * i + 2]
        scores = dot(k, q, NT)
        cum_row = cum_ref[h : h + 1, :]
        soft, mix = [], []
        for j in range(tiles):
            s = scores[j * BLK : (j + 1) * BLK]
            causal = row <= col - j * BLK
            soft.append(jnp.where(causal & (row >= thr_ref[own + j : own + j + 1, :]), s, NEG))
            gap = cum_row - cumt_ref[j * BLK : (j + 1) * BLK, h : h + 1]
            ok = causal & (row >= start_ref[0:1, :] - j * BLK)
            decay = jnp.exp(jnp.where(ok, gap, NEG))
            mix.append((s * decay * (1.0 / divisor)).astype(jnp.bfloat16))
        top, total, weights = softmax_of(soft, scale2)
        rows = slice(i * 128, (i + 1) * 128)
        o_ref[rows, :] = dot(v, jnp.concatenate(weights, axis=0), TN)
        lin_ref[rows, :] = dot(v, jnp.concatenate(mix, axis=0), TN)
        top_ref[i : i + 1, :] = top
        tot_ref[i : i + 1, :] = total
    token_ref[...] = jnp.zeros_like(token_ref)


def partial_softmax(q, groups, thr, scale2):
    tiles = groups[0][1].shape[0] // BLK
    row = lax.broadcasted_iota(jnp.int32, (BLK, q.shape[0]), 0)
    parts = []
    for first, keys, _ in groups:
        scores = dot(keys, q, NT)
        for j in range(tiles):
            ok = row >= thr[first + j : first + j + 1]
            parts.append(jnp.where(ok, scores[j * BLK : (j + 1) * BLK], NEG))
    top, total, weights = softmax_of(parts, scale2)
    o = None
    for g, (_, _, values) in enumerate(groups):
        here = dot(values, jnp.concatenate(weights[g * tiles : (g + 1) * tiles], axis=0), TN)
        o = here if o is None else o + here
    return top, total, o


def earlier_kernel(scale2, n, token_in, q_ref, thr_ref, two, od_ref, topd_ref, totd_ref, o_ref, top_ref, tot_ref, token_ref):
    length = q_ref.shape[0]
    thr = thr_ref[...]
    for i in range(n):
        rows = slice(i * 128, (i + 1) * 128)
        keys = two[0:length, i * 128 : (i + 1) * 128]
        values = two[0:length, (n + i) * 128 : (n + i + 1) * 128]
        top, total, o = partial_softmax(q_ref[:, rows], [(0, keys, values)], thr, scale2)
        top_d = topd_ref[i : i + 1, :]
        new_top = jnp.maximum(top, top_d)
        a, b = jnp.exp2(top - new_top), jnp.exp2(top_d - new_top)
        o_ref[rows, :] = o * a + od_ref[rows, :] * b
        top_ref[i : i + 1, :] = new_top
        tot_ref[i : i + 1, :] = total * a + totd_ref[i : i + 1, :] * b
    token_ref[...] = jnp.zeros_like(token_ref)


class Pieces:
    def __init__(self, n, two, even, odd, entry, even_at, even_dec):
        self.n, self.two, self.even, self.odd, self.even_at = n, two, even, odd, even_at
        length = self.length = odd.shape[0] - 16
        rows2 = two[length:, 0:length].astype(jnp.float32)
        rows1 = (even[even_dec : even_dec + 16, 0:length] + odd[length:, 0:length]).astype(jnp.float32)
        self.tot1 = [join2(rows1, 2 * n + 2 * i) for i in range(n)]
        self.tot2 = [join2(rows2, 2 * n + 2 * i) for i in range(n)]
        after1 = [join2(rows1, 2 * i) for i in range(n)]
        after2 = [join2(rows2, 2 * i) + self.tot1[i] for i in range(n)]
        col = lax.broadcasted_iota(jnp.int32, (1, length), 1)
        w1 = [jnp.where(col - length >= entry, jnp.exp(x), 0.0) for x in after1]
        w2 = [jnp.where(col - 2 * length >= entry, jnp.exp(x), 0.0) for x in after2]
        self.weight = stack_rows(w1 + w2, BLK, length).T

    def part(self, index):
        cols = slice(index * 128, (index + 1) * 128)
        at = slice(self.even_at + index * 128, self.even_at + (index + 1) * 128)
        return self.two[0 : self.length, cols], self.even[0 : self.length, at] + self.odd[0 : self.length, cols]

    def attend(self, i, q, thr, scale2, both=True):
        tiles = self.length // BLK
        k2, k1 = self.part(i)
        v2, v1 = self.part(self.n + i)
        groups = [(0, k2, v2), (tiles, k1, v1)] if both else [(tiles, k1, v1)]
        top, total, o = partial_softmax(q, groups, thr, scale2)
        n = self.n
        kw1 = (k1.astype(jnp.float32) * self.weight[:, i : i + 1]).astype(jnp.bfloat16)
        kw2 = (k2.astype(jnp.float32) * self.weight[:, n + i : n + i + 1]).astype(jnp.bfloat16)
        state = dot(v2, kw2, TN) + dot(v1, kw1, TN)
        return top, total, o, state.astype(jnp.bfloat16)


def far_thresholds(keep_ref, ahead_ref):
    keep = keep_ref[...].astype(jnp.float32)
    tiles = keep.shape[1] // BLK
    thr = []
    for j in range(2 * tiles):
        base = (j - REACH * tiles) * BLK
        thr.append(jnp.where(keep[j : j + 1] > 0.5, ahead_ref[0:1, :] - base, FAR_OFF))
    return jnp.concatenate(thr, axis=0)


def far_earlier_kernel(scale2, n, token_in, q_ref, keep_ref, ahead_ref, two, o_ref, top_ref, tot_ref, token_ref):
    thr = far_thresholds(keep_ref, ahead_ref)
    length = thr.shape[1]
    for i in range(n):
        rows = slice(i * 128, (i + 1) * 128)
        keys = two[0:length, i * 128 : (i + 1) * 128]
        values = two[0:length, (n + i) * 128 : (n + i + 1) * 128]
        top, total, o = partial_softmax(q_ref[0:length, rows], [(0, keys, values)], thr, scale2)
        o_ref[rows, :] = o
        top_ref[i : i + 1, :] = top
        tot_ref[i : i + 1, :] = total
    token_ref[...] = jnp.zeros_like(token_ref)


def far_kernel(scale2, n, both, even_at, even_dec, token_in, entry_ref, q_ref, keep_ref, ahead_ref, two, even, odd, *rest):
    out_ref, token_ref = rest[-2:]
    p = Pieces(n, two, even, odd, entry_ref[0:1, :], even_at, even_dec)
    length = p.length
    thr = far_thresholds(keep_ref, ahead_ref)
    rows = [jnp.ones((1, length), jnp.float32)]
    for i in range(n):
        top, total, o, state = p.attend(i, q_ref[0:length, i * 128 : (i + 1) * 128], thr, scale2, both)
        if not both:
            o_e, top_e, tot_e = rest[0][i * 128 : (i + 1) * 128, :], rest[1][i : i + 1, :], rest[2][i : i + 1, :]
            new_top = jnp.maximum(top, top_e)
            a, b = jnp.exp2(top - new_top), jnp.exp2(top_e - new_top)
            top, total, o = new_top, total * a + tot_e * b, o * a + o_e * b
        r = i * 128
        out_ref[r : r + 128, 0:length] = (o * (1.0 / total)).astype(jnp.bfloat16)
        out_ref[r : r + 128, length:] = state
        lse = top + jnp.log(total) * LOG2E
        rows += list(split3(lse))
    out_ref[n * 128 :, 0:length] = stack_rows(rows, 16, length).astype(jnp.bfloat16)
    out_ref[n * 128 :, length:] = jnp.zeros((16, 128), jnp.bfloat16)
    token_ref[...] = jnp.zeros_like(token_ref)


def near_kernel(
    scale2, n, first, both, even_at, even_dec, token_in, entry_ref, q_ref, thr_ref, coef_ref, two, even, odd, od_ref, topd_ref, totd_ref, lind_ref,
    x_ref, on_ref, st_ref, token_ref,
):
    entry = entry_ref[0:1, :]
    p = Pieces(n, two, even, odd, entry, even_at, even_dec)
    length = p.length
    lses, coefs = [], []
    thr = thr_ref[...]
    for i in range(n):
        q = q_ref[:, i * 128 : (i + 1) * 128]
        rows = slice(i * 128, (i + 1) * 128)
        top, total, o, state = p.attend(i, q, thr, scale2, both)
        top_d = topd_ref[i : i + 1, :]
        new_top = jnp.maximum(top, top_d)
        a, b = jnp.exp2(top - new_top), jnp.exp2(top_d - new_top)
        total = total * a + totd_ref[i : i + 1, :] * b
        inv = 1.0 / total
        on = o * (a * inv) + od_ref[rows, :] * (b * inv)
        coef = coef_ref[first + i : first + i + 1, :]
        x_ref[rows, :] = lind_ref[rows, :] + dot(state, q, NT) * coef + on
        on_ref[rows, :] = on
        lses.append(new_top + jnp.log(total) * LOG2E)
        through = jnp.where(entry < -2 * length, jnp.exp(p.tot1[i] + p.tot2[i]), 0.0)
        coefs.append(coef * through)
    st_ref[...] = stack_rows(lses + coefs, 8, length)
    token_ref[...] = jnp.zeros_like(token_ref)


def merge_kernel(n, token_in, q_ref, pay_ref, x_ref, on_ref, st_ref, mixed_ref, sq_ref, token_ref):
    squares = None
    length = q_ref.shape[0]
    stats = pay_ref[n * 128 :, 0:length].astype(jnp.float32)
    for i in range(n):
        q = q_ref[:, i * 128 : (i + 1) * 128]
        rows = slice(i * 128, (i + 1) * 128)
        lse_far = join3(stats, 1 + 3 * i)
        far = pay_ref[rows, 0:length].astype(jnp.float32)
        share = 1.0 / (1.0 + jnp.exp2(jnp.minimum(st_ref[i : i + 1, :] - lse_far, 120.0)))
        share = jnp.where((lse_far > 0.5 * NEG) & (stats[0:1] > 0.5), share, 0.0)
        lin = dot(pay_ref[rows, length:], q, NT) * st_ref[n + i : n + i + 1, :]
        mixed = x_ref[rows, :] + share * (far - on_ref[rows, :]) + lin
        mixed_ref[:, rows] = mixed.T
        part = jnp.sum(mixed * mixed, axis=0, keepdims=True)
        squares = part if squares is None else squares + part
    sq_ref[...] = squares
    token_ref[...] = jnp.zeros_like(token_ref)


def norm_kernel(parts, *refs):
    mixed_refs, sq_ref, gain_ref, out_ref = refs[:parts], refs[parts], refs[parts + 1], refs[parts + 2]
    inverse = lax.rsqrt(jnp.sum(sq_ref[...], axis=0, keepdims=True) / D + EPSILON)
    spread = (jnp.zeros((128, inverse.shape[1]), jnp.float32) + inverse).T
    col = 0
    for ref in mixed_refs:
        for i in range(ref.shape[1] // 128):
            part = ref[:, i * 128 : (i + 1) * 128] * spread
            out_ref[:, col : col + 128] = (part * gain_ref[:, col : col + 128]).astype(jnp.bfloat16)
            col += 128


def on_device(query, key, value, log_decay, doc_lengths, tile_mask, gain):
    length, features = query.shape
    heads = log_decay.shape[0]
    hd = features // heads
    tiles = length // BLK
    sizes = [(heads + 2) // 3, (heads + 1) // 3, heads // 3]
    firsts = [sum(sizes[:c]) for c in range(len(sizes))]
    divisor = hd * math.sqrt(length)
    scale2 = LOG2E / math.sqrt(hd)
    f32, bf16 = jnp.float32, jnp.bfloat16
    shape = jax.ShapeDtypeStruct
    loose = pl.BlockSpec(memory_space=pl.ANY)
    hbm = pl.BlockSpec(memory_space=pltpu.HBM)
    dma = pltpu.SemaphoreType.DMA

    def whole(x):
        return pl.BlockSpec(x.shape, lambda *_: (0,) * len(x.shape))

    def cols(c, rows=length):
        return pl.BlockSpec((rows, sizes[c] * hd), lambda *_: (0, firsts[c] // sizes[c]))

    def run(kernel, name, us, specs, args, outs, scratch=(), limit=24, out_specs=None):
        outs = outs + [shape((8, 128), f32)]
        out_specs = (out_specs or [whole(o) for o in outs[:-1]]) + [whole(outs[-1])]
        return pl.pallas_call(
            kernel,
            grid=(1,),
            in_specs=specs,
            out_specs=out_specs,
            out_shape=outs,
            scratch_shapes=scratch,
            compiler_params=params(limit),
            cost_estimate=pl.CostEstimate(flops=0, bytes_accessed=int(us * 3.69e6), transcendentals=0),
            name=name,
        )(*args)

    def pay_shape(c):
        return shape((length + 16, max(length, 2 * sizes[c] * hd)), bf16)

    docs = doc_lengths[None, :]
    outs = [
        shape(((REACH + 1) * tiles, length), jnp.int32),
        shape((8, length), jnp.int32),
        shape((8, length), jnp.int32),
        shape((8, length), jnp.int32),
        shape((16, length), bf16),
        shape((heads, length), f32),
        shape((length, BLK), f32),
        shape((heads, length), f32),
        shape((16 * len(sizes), length), bf16),
    ]
    pay0, token = run(
        partial(first_kernel, sizes[0]),
        "first_chunk",
        1,
        [hbm, hbm, hbm],
        (log_decay, key, value),
        [pay_shape(0)],
        [pltpu.VMEM(log_decay.shape, f32), pltpu.VMEM(pay_shape(0).shape, bf16), dma((6,))],
        limit=60,
        out_specs=[hbm],
    )
    thr, start, ahead, entry, keep, cum, cum_t, coef, dec, token = run(
        partial(prep_kernel, divisor, sizes),
        "prep",
        2,
        [loose, whole(docs), whole(tile_mask), whole(log_decay)],
        (token, docs, tile_mask, log_decay),
        outs,
    )
    thr_near = pl.BlockSpec((2 * tiles, length), lambda *_: (1, 0))

    def own(c, token, *after):
        n, first = sizes[c], firsts[c]
        outs = [shape((n * hd, length), f32), shape((n, length), f32), shape((n, length), f32), shape((n * hd, length), f32)]

        def kernel(*refs):
            own_kernel(scale2, divisor, n, first, *refs[len(after) + 1 :])

        *result, token = run(
            kernel,
            "own_piece",
            n * 0.8,
            [loose] * (len(after) + 1) + [hbm] * 3 + [whole(thr), whole(start), whole(cum), whole(cum_t)],
            (*after, token, query, key, value, thr, start, cum, cum_t),
            outs,
            [pltpu.VMEM((3 * n, length, hd), bf16), dma((3 * n,))],
        )
        return result, token

    width1 = pay_shape(1).shape[1]

    def kv(c):
        return two_back[c], from_even[min(c, 1)], from_odd[c]

    def even_place(c):
        return (0, length) if c < 2 else (width1, length + 16)

    def near(c, token):
        n = sizes[c]
        args = (*kv(c), *diag[c])
        x, on, st, token = run(
            partial(near_kernel, scale2, n, firsts[c], c != 1, *even_place(c)),
            "near_pieces",
            1.8 * n,
            [loose, whole(entry), cols(c), thr_near, whole(coef)] + [whole(a) for a in args],
            (token, entry, query, thr, coef, *args),
            [shape((n * hd, length), f32), shape((n * hd, length), f32), shape((8, length), f32)],
        )
        return (x, on, st), token

    def earlier(c, token):
        n = sizes[c]
        args = (two_back[c], *diag[c][:3])
        o, top, tot, token = run(
            partial(earlier_kernel, scale2, n),
            "earlier_piece",
            0.8 * n,
            [loose, cols(c), thr_near] + [whole(a) for a in args],
            (token, query, thr, *args),
            [shape((n * hd, length), f32), shape((n, length), f32), shape((n, length), f32)],
        )
        diag[c] = [o, top, tot, diag[c][3]]
        return token

    kept = pl.BlockSpec((16, length), lambda *_: (length // 16, 0))

    def far_earlier(c, token):
        n = sizes[c]
        *first, token = run(
            partial(far_earlier_kernel, scale2, n),
            "far_earlier",
            0.7 * n,
            [loose, cols(c), kept, whole(ahead), whole(two_back[c])],
            (token, q_far, q_far, ahead, two_back[c]),
            [shape((n * hd, length), f32), shape((n, length), f32), shape((n, length), f32)],
        )
        return first, token

    def far(c, token, first=()):
        n = sizes[c]
        args = (*kv(c), *first)
        pay, token = run(
            partial(far_kernel, scale2, n, not first, *even_place(c)),
            "far_pieces",
            1.5 * n,
            [loose, whole(entry), cols(c), kept, whole(ahead)] + [whole(a) for a in args],
            (token, entry, q_far, q_far, ahead, *args),
            [shape((n * hd + 16, length + hd), bf16)],
        )
        return shifted(pay, 2), token

    def merge(c, token):
        n = sizes[c]
        args = (pays[c], *parts[c])
        return run(
            partial(merge_kernel, n),
            "merge",
            0.5 * n,
            [loose, cols(c)] + [whole(a) for a in args],
            (token, query, *args),
            [shape((length, n * hd), f32), shape((1, length), f32)],
        )

    def gate(x, *after):
        return pl.pallas_call(
            gate_kernel,
            in_specs=[loose] * (1 + len(after)),
            out_specs=loose,
            out_shape=shape(x.shape, x.dtype),
            input_output_aliases={0: 0},
            compiler_params=params(1),
            name="gate",
        )(x, *after)

    chunks = range(len(sizes))
    diag, parts, pays = [None] * 3, [None] * 3, [None] * 3
    two_back, from_even, from_odd = [None] * 3, [None] * 2, [None] * 3
    two_back[0] = shifted(pay0, 2)
    from_even[0] = even_to_odd(pay0)
    diag[0], token = own(0, token)
    one, both, q_pay, token = run(
        partial(pack_kernel, sizes, width1),
        "pack",
        3,
        [loose, hbm, whole(keep), hbm, hbm, whole(dec)],
        (token, query, keep, key, value, dec),
        [pay_shape(1), shape((length + 32, width1 + pay_shape(2).shape[1]), bf16), shape((length + 16, features), bf16)],
        [dma((7,))],
    )
    two_back[1] = shifted(one, 2)
    from_odd[0] = odd_to_even(two_back[0])
    q_far = shifted(q_pay, -2)
    diag[1], token = own(1, token, two_back[0])
    dec_rows = pl.BlockSpec((16, length), lambda *_: (2, 0))
    pay, token = run(
        partial(pack_last_kernel, sizes), "pack", 1, [loose, hbm, hbm, dec_rows], (token, key, value, dec), [pay_shape(2)], [dma((2,))]
    )
    two_back[2] = shifted(pay, 2)
    from_even[1] = even_to_odd(both)
    from_odd[1] = odd_to_even(two_back[1])
    diag[2], token = own(2, token)
    pays[0], token = far(0, token)
    parts[0], token = near(0, token)
    two_back[2] = gate(two_back[2], token)
    from_odd[2] = odd_to_even(two_back[2])
    first, token = far_earlier(1, token)
    token = earlier(1, token)
    pays[1], token = far(1, token, first)
    pays[2], token = far(2, token)
    parts[1], token = near(1, token)
    parts[2], token = near(2, token)
    mixed, total = [], None
    for c in chunks:
        m, s, token = merge(c, token)
        mixed.append(m)
        total = s if total is None else total + s
    ranks = lax.axis_size("head")
    everyone = lax.all_gather(total.reshape(length // 128, 128), "head").reshape(ranks, length)
    gain = gain[None, :]
    return pl.pallas_call(
        partial(norm_kernel, len(mixed)),
        grid=(1,),
        in_specs=[whole(m) for m in mixed] + [whole(everyone), whole(gain)],
        out_specs=whole(query),
        out_shape=shape((length, features), bf16),
        compiler_params=params(),
        name="normalize",
    )(*mixed, everyone, gain)


def solution(mesh):
    placed = (
        P("ctx", "head"),
        P("ctx", "head"),
        P("ctx", "head"),
        P("head", "ctx"),
        P(),
        P("ctx", None),
        P("head"),
    )
    return jax.shard_map(on_device, mesh=mesh, in_specs=placed, out_specs=P("ctx", "head"), check_vma=False)
```
